512 devices in a mesh: frame: 64 (over z, x), head: 4 (over y_hi, core), dp: 2 (over y_lo).
Axes of the slice: x: 4, y: 4 (y_hi: 2, y_lo: 2; y = y_hi * 2 + y_lo), z: 16, core: 2. Of those that a mesh axis runs over, the one named last changes fastest.
Arguments:
- inputs: bfloat16 [128, 128, 1152], P(('dp', 'frame')), parts along dimension 0, may hold values from -6 to 6
- modulation: float32 [6, 1152], P('dp'), parts along dimension 0, may hold values from -3 to 3
- qkv_weight: bfloat16 [3, 1152, 1152], P(None, 'frame', 'head'), may hold values from -0.1875 to 0.1875
- proj_weight: bfloat16 [1152, 1152], P('head', 'frame'), may hold values from -0.1875 to 0.1875
- q_gain: float32 [72], replicated, may hold values from 0.5 to 10
- k_gain: float32 [72], replicated, may hold values from 0.5 to 10
- cotangent: bfloat16 [128, 128, 1152], P(('dp', 'frame')), parts along dimension 0, may hold values from -16 to 16
Outputs:
- output: bfloat16 [128, 128, 1152], P(('dp', 'frame')), parts along dimension 0
- input_grad: bfloat16 [128, 128, 1152], P(('dp', 'frame')), parts along dimension 0
- proj_grad: float32 [2304, 1152], P(('dp', 'head'), 'frame'), parts along dimension 0
The draws below stay inside these ranges and needn't reach their ends.
There are 2 independent parts, one for each index of `dp`. The reference program is written for one: setup_inputs(seed, part) draws one part's arguments, and reference() takes and returns one part's arrays. A program takes and returns all parts, laid end to end along the dimension named above; an argument that names none is the same for every part. Nothing has to cross between parts.
All inputs are finite; a program needn't handle non-finite values.
Results may differ from the reference program's by a relative error of at most 0.015.
The reference program's roundings to bfloat16 on the way count: a program that leaves them out, or rounds other values in their place, can miss the bound.
Values may be sent and summed in bfloat16 or wider, within the bound.
A program may use at most 64 MiB of HBM per device.

```python
import jax
import jax.numpy as jnp
from jax import lax

HEADS = 16
HEAD_DIM = 72
D = 1152
SPATIAL = 128
FRAMES = 64


def gain_draw(key, lo_val, hi_val):
    lo_log = jnp.log(jnp.float32(lo_val))
    hi_log = jnp.log(jnp.float32(hi_val))
    return jnp.exp(jax.random.uniform(key, (HEAD_DIM,), jnp.float32, lo_log, hi_log))


def draw_q_gain(key, part):
    key = jax.random.fold_in(key, 11)
    return gain_draw(key, 0.7, 2.5)


def draw_k_gain(key, part):
    key = jax.random.fold_in(key, 23)
    return gain_draw(key, 0.7, 2.5)


def with_spikes(result, key, source, target, blocks, factor):
    def block_of(axis_at):
        return (jnp.arange(result.shape[axis_at]) // (result.shape[axis_at] // blocks)).reshape((-1,) + (1,) * (result.ndim - 1 - axis_at))

    near = jax.random.permutation(key, blocks)[block_of(target)]
    far = (block_of(target) + blocks // 2) % blocks
    return jnp.where((block_of(source) == near) | (block_of(source) == far), factor * result, result)


def block_levels(rng, shape, shards, least, largest):
    def one(dim, shards_of):
        heights = jax.random.uniform(jax.random.fold_in(jax.random.fold_in(rng, 6), dim), (shards_of,), jnp.float32, least / len(shards), largest / len(shards))
        return jnp.repeat(jnp.exp(heights), shape[dim] // shards_of).reshape((-1,) + (1,) * (len(shape) - dim - 1))

    level = one(*shards[0])
    for cut in shards[1:]:
        level = level * one(*cut)
    return level


def gaussian(key, shape, width, most, split=(), kind=jnp.bfloat16):
    drawn = jax.random.normal(key, shape, jnp.float32) * width
    if len(split) > 0:
        drawn = block_levels(key, shape, split, -0.22, 0.18) * drawn
    return jnp.clip(drawn, min=-most, max=most).astype(kind)


def bell_draw_with(own_key, dims, deviation, bound, pieces, heavy, dtype=jnp.bfloat16):
    result = deviation * jax.random.normal(own_key, dims, jnp.float32)
    if pieces:
        result = result * block_levels(own_key, dims, pieces, -0.22, 0.18)
    return jnp.clip(with_spikes(result, jax.random.fold_in(own_key, 3), *heavy), -bound, bound).astype(dtype)


def setup_inputs(seed: int = 0, part: int = 0) -> dict:
    splits = jax.random.split(jax.random.key(seed), 8)
    own_keys = jax.random.split(jax.random.fold_in(splits[7], part), 8)
    return {
        "inputs": gaussian(own_keys[0], (FRAMES, SPATIAL, D), 1.0, 6.0, ((0, 64),)),
        "modulation": gaussian(own_keys[1], (3, D), 0.7, 3.0, (), jnp.float32),
        "qkv_weight": gaussian(splits[2], (3, D, D), D ** -0.5, 0.1875, ((1, 64), (2, 4))),
        "proj_weight": gaussian(splits[3], (D, D), D ** -0.5, 0.1875, ((0, 4), (1, 64))),
        "q_gain": draw_q_gain(jax.random.fold_in(splits[7], 71), part),
        "k_gain": draw_k_gain(jax.random.fold_in(splits[7], 71), part),
        "cotangent": bell_draw_with(own_keys[6], (FRAMES, SPATIAL, D), 1.0, 16.0, ((0, 64),), (0, 2, 64, 4.0)),
    }


def head_norm(raw_part, gain_vec):
    inv_root = 1.0 / jnp.sqrt(lax.optimization_barrier(jnp.mean(raw_part * raw_part, axis=-1, keepdims=True)) + 1e-06)
    return ((raw_part * inv_root * gain_vec).astype(jnp.bfloat16), inv_root)

def head_norm_back(raw_part, inv_root, gain_vec, d_normed):
    scaled = gain_vec * d_normed.astype(jnp.float32)
    inner = lax.optimization_barrier(jnp.mean(raw_part * scaled, axis=-1, keepdims=True))
    return (inv_root * scaled - raw_part * inv_root ** 3 * inner).astype(jnp.bfloat16)

def reference(inputs, modulation, qkv_weight, proj_weight, q_gain, k_gain, cotangent):
    tok_rows = FRAMES * SPATIAL
    inputs_f = inputs.reshape(tok_rows, D).astype(jnp.float32)
    shift_vec, scale_vec, gate_vec = (modulation[0], modulation[1], modulation[2])
    center = lax.optimization_barrier(jnp.mean(inputs_f, axis=1, keepdims=True))
    centered = inputs_f - center
    rstd_col = 1.0 / jnp.sqrt(lax.optimization_barrier(jnp.mean(centered * centered, axis=1, keepdims=True)) + 1e-06)
    normed = centered * rstd_col
    hidden_in = (normed * (1.0 + scale_vec) + shift_vec).astype(jnp.bfloat16)
    raw_proj = jnp.einsum('rd,wde->wre', hidden_in.astype(jnp.float32), qkv_weight.astype(jnp.float32))
    raw_query = raw_proj[0].reshape(tok_rows, HEADS, HEAD_DIM)
    raw_key = raw_proj[1].reshape(tok_rows, HEADS, HEAD_DIM)
    query, root_q = head_norm(raw_query, q_gain)
    key_n, root_k = head_norm(raw_key, k_gain)
    value = raw_proj[2].astype(jnp.bfloat16)
    shape4 = (FRAMES, SPATIAL, HEADS, HEAD_DIM)
    query_f = query.reshape(shape4).astype(jnp.float32)
    key_f = key_n.reshape(shape4).astype(jnp.float32)
    value_f = value.reshape(shape4).astype(jnp.float32)
    factor = 1.0 / jnp.sqrt(jnp.float32(HEAD_DIM))
    scores = jnp.einsum('fshd,gshd->shfg', query_f, key_f) * factor
    peak = lax.optimization_barrier(jnp.max(scores, axis=-1, keepdims=True))
    expo = jnp.exp(scores - peak)
    probs = expo / lax.optimization_barrier(jnp.sum(expo, axis=-1, keepdims=True))
    probs_b = probs.astype(jnp.bfloat16).astype(jnp.float32)
    attended = jnp.einsum('shfg,gshd->fshd', probs_b, value_f).astype(jnp.bfloat16).reshape(tok_rows, D)
    branch = jnp.dot(attended, proj_weight, preferred_element_type=jnp.float32)
    output = (inputs_f + gate_vec * branch).astype(jnp.bfloat16)
    d_out = cotangent.reshape(tok_rows, D).astype(jnp.float32)
    d_branch = (gate_vec * d_out).astype(jnp.bfloat16)
    proj_grad = jnp.dot(attended.T, d_branch, preferred_element_type=jnp.float32)
    d_att = jnp.dot(d_branch, proj_weight.T, preferred_element_type=jnp.float32).astype(jnp.bfloat16)
    d_att_f = d_att.reshape(shape4).astype(jnp.float32)
    d_value = jnp.einsum('shfg,fshd->gshd', probs_b, d_att_f).astype(jnp.bfloat16)
    d_probs = jnp.einsum('fshd,gshd->shfg', d_att_f, value_f)
    d_scores = (probs * (d_probs - lax.optimization_barrier(jnp.sum(probs * d_probs, axis=-1, keepdims=True))) * factor).astype(jnp.bfloat16).astype(jnp.float32)
    d_query = jnp.einsum('shfg,gshd->fshd', d_scores, key_f).astype(jnp.bfloat16)
    d_key = jnp.einsum('shfg,fshd->gshd', d_scores, query_f).astype(jnp.bfloat16)
    d_raw_q = head_norm_back(raw_query, root_q, q_gain, d_query.reshape(tok_rows, HEADS, HEAD_DIM))
    d_raw_k = head_norm_back(raw_key, root_k, k_gain, d_key.reshape(tok_rows, HEADS, HEAD_DIM))
    d_raw = jnp.stack([d_raw_q.reshape(tok_rows, D), d_raw_k.reshape(tok_rows, D), d_value.reshape(tok_rows, D)])
    d_hidden = jnp.einsum('wre,wde->rd', d_raw.astype(jnp.float32), qkv_weight.astype(jnp.float32))
    d_normed = d_hidden * (1.0 + scale_vec)
    d_in = rstd_col * (d_normed - lax.optimization_barrier(jnp.mean(d_normed, axis=1, keepdims=True)) - normed * lax.optimization_barrier(jnp.mean(d_normed * normed, axis=1, keepdims=True)))
    input_grad = (d_out + d_in).astype(jnp.bfloat16)
    return (output.reshape(FRAMES, SPATIAL, D), input_grad.reshape(FRAMES, SPATIAL, D), proj_grad)
```

```python
import jax
import jax.numpy as jnp
import numpy as np
from jax import lax
from jax.experimental import pallas as pl
from jax.experimental.pallas import tpu as pltpu
from jax.sharding import PartitionSpec as P

MESH = pl.DeviceIdType.MESH
BF = jnp.bfloat16
F32 = jnp.float32
NZ, NX, NY = 16, 4, 4
HD = 72
FPAD = 320
WCOLS = 576

S_WX = 0
S_RR = S_WX + 3
S_RL = S_RR + 8
S_X1 = S_RL + 7
S_Z1 = S_X1 + 3
S_AY = S_Z1 + 15
S_AC = S_AY + 3
S_B = S_AC + 4
S_H = S_B + 4
S_Z2 = S_H + 4
S_X2 = S_Z2 + 15
S_OY = S_X2 + 3
S_OC = S_OY + 1
S_PX = S_OC + 2
S_PZ = S_PX + 3
S_PY = S_PZ + 15
N_SEM = S_PY + 1


def one_hot(shape, pairs):
    m = np.zeros(shape, np.float32)
    for r, c in pairs:
        m[r, c] = 1.0
    return m.astype(jnp.bfloat16)


def selections():
    r2, r4, r16, r18, r72 = range(2), range(4), range(16), range(18), range(72)
    return [
        one_hot((80, 128), [(x * 18 + j, x * 32 + j) for x in r4 for j in r18]),
        one_hot((WCOLS, 1024), [(g * 72 + j, g * 128 + j) for g in range(8) for j in r72]),
        one_hot((256, 256), [(z * 16 + a * 8 + x * 2 + i, x * 64 + z * 4 + a * 2 + i) for z in r16 for x in r4 for a in r2 for i in r2]),
        one_hot((256, 256), [(a * 128 + z * 8 + x * 2 + i, z * 16 + a * 8 + x * 2 + i) for z in r16 for x in r4 for a in r2 for i in r2]),
        one_hot((256, 256), [(x * 64 + a * 32 + z * 2 + i, z * 16 + a * 8 + x * 2 + i) for z in r16 for x in r4 for a in r2 for i in r2]),
        one_hot((256, 256), [(a * 128 + z * 8 + x * 2 + i, x * 64 + a * 32 + z * 2 + i) for z in r16 for x in r4 for a in r2 for i in r2]),
        one_hot((FPAD, 288), [(g * 80 + j, g * 72 + j) for g in r4 for j in r72]),
        one_hot((FPAD, FPAD), [(z * 80 + x * 18 + j, x * 80 + z * 18 + j) for z in r4 for x in r4 for j in r18]),
        one_hot((128, 80), [(z * 32 + j, z * 18 + j) for z in r4 for j in r18]),
        one_hot((256, 288), [(h * 128 + j, h * 72 + j) for h in r2 for j in r72]),
        one_hot((256, 288), [(h * 128 + j, 144 + h * 72 + j) for h in r2 for j in r72]),
    ]


def dot(a, b):
    return jnp.dot(a, b, preferred_element_type=F32)


def dot_nt(a, b):
    return lax.dot_general(a, b, (((1,), (1,)), ((), ())), preferred_element_type=F32)


def dot_tn(a, b):
    return lax.dot_general(a, b, (((0,), (0,)), ((), ())), preferred_element_type=F32)


def mod(a, n):
    return lax.rem(a + n, n)


def kernel(
    w_in, rows_in, qg_ref, kg_ref, sel80, place, p_x1, p_z1, p_z2, p_x2, unpad, p_pg, p_pz, p_h0, p_h1,
    out_ref, pg_ref,
    xb, g, wp, r1, z1, r2, a, bp, bq, bt, bu, hp, hq, ht, hu, zb, r3, xs, r4, oa, px, pxr, pz, pzr, pgs,
    ss, rs,
):
    f, hd, dp = lax.axis_index("frame"), lax.axis_index("head"), lax.axis_index("dp")
    z, x = f // NX, lax.rem(f, NX)
    core, y = lax.rem(hd, 2), (hd // 2) * 2 + dp

    def at_x(d):
        return (z * NX + mod(x + d, NX), hd, dp)

    def at_z(d):
        return (mod(z + d, NZ) * NX + x, hd, dp)

    def at_y(d):
        yy = mod(y + d, NY)
        return (f, (yy // 2) * 2 + core, lax.rem(yy, 2))

    across = (f, hd + 1 - 2 * core, dp)

    def copy(src, dst, i, dev):
        return pltpu.make_async_remote_copy(
            src_ref=src, dst_ref=dst, send_sem=ss.at[i], recv_sem=rs.at[i], device_id=dev, device_id_type=MESH
        )

    sends = []

    def send(*args):
        c = copy(*args)
        c.start()
        sends.append(c)

    def landed(ref, i):
        copy(ref, ref, i, across).wait_recv()

    barrier = pltpu.get_barrier_semaphore()

    def greet(dev):
        pl.semaphore_signal(barrier, inc=1, device_id=dev, device_id_type=MESH)

    with jax.named_scope("greet"):
        for d in range(1, NX):
            greet(at_x(d))
        for d in range(1, NY):
            greet(at_y(d))
        greet(across)

        def greet_z(d, c):
            greet(at_z(d))
            return c

        lax.fori_loop(1, NZ, greet_z, 0)
        pl.semaphore_wait(barrier, 22)

    def z_send(src, dst, base):
        def step(d, c):
            copy(src.at[mod(z + d, NZ)], dst.at[z], base + d - 1, at_z(d)).start()
            return c

        lax.fori_loop(1, NZ, step, 0)

    def z_landed(dst, base):
        def step(d, c):
            landed(dst.at[mod(z - d, NZ)], base + d - 1)
            return c

        lax.fori_loop(1, NZ, step, 0)

    def z_sent(src, dst, base):
        def step(d, c):
            copy(src.at[mod(z + d, NZ)], dst.at[z], base + d - 1, at_z(d)).wait_send()
            return c

        lax.fori_loop(1, NZ, step, 0)

    with jax.named_scope("along_x"):
        for d in range(1, NX):
            send(w_in, xb.at[x], S_WX + d - 1, at_x(d))
        for d in range(1, NX):
            send(rows_in.at[mod(x + d, NX)], r1.at[x], S_X1 + d - 1, at_x(d))
        xb[x] = w_in[...]
        r1[x] = rows_in[x]
        for d in range(1, NX):
            landed(xb.at[mod(x - d, NX)], S_WX + d - 1)
        g[z] = dot(sel80[...], xb[...].reshape(128, WCOLS)).astype(BF)

    def put(c):
        wp[c] = dot(g[c], place[...]).astype(BF)

    def right(s):
        c = mod(z - s + 1, NZ)
        return copy(g.at[c], g.at[c], S_RR + s - 1, at_z(1))

    def left(s):
        c = mod(z + s - 1, NZ)
        return copy(g.at[c], g.at[c], S_RL + s - 1, at_z(-1))

    def ring(lo, hi):
        def step(s, c):
            right(s).start()
            left(s).start()
            put(mod(z - s + 1, NZ))
            put(mod(z + s - 1, NZ))
            landed(g.at[mod(z - s, NZ)], S_RR + s - 1)
            landed(g.at[mod(z + s, NZ)], S_RL + s - 1)
            return c

        lax.fori_loop(lo, hi, step, 0)

    with jax.named_scope("ring_a"):
        ring(1, 2)
    with jax.named_scope("rows_x"):
        for d in range(1, NX):
            landed(r1.at[mod(x - d, NX)], S_X1 + d - 1)
        z1[...] = dot(p_x1[...], r1[...].reshape(256, FPAD)).astype(BF).reshape(NZ, 16, FPAD)
        z_send(z1, r2, S_Z1)
        r2[z] = z1[z]
    with jax.named_scope("ring_b"):
        ring(2, 4)
    with jax.named_scope("rows_z"):
        z_landed(r2, S_Z1)
        a[core, y] = dot(p_z1[...], r2[...].reshape(256, FPAD)).astype(BF)
        for d in range(1, NY):
            send(a.at[core, y], a.at[core, y], S_AY + d - 1, at_y(d))
        send(a.at[core, y], a.at[core, y], S_AC, across)
    with jax.named_scope("ring_c"):
        ring(4, 7)
    with jax.named_scope("rows_y"):
        for d in range(1, NY):
            slot = a.at[core, mod(y - d, NY)]
            landed(slot, S_AY + d - 1)
            send(slot, slot, S_AC + d, across)
    with jax.named_scope("ring_d"):
        ring(7, 8)
        right(8).start()
        put(mod(z - 7, NZ))
        put(mod(z + 7, NZ))
        for d in range(NY):
            landed(a.at[1 - core, mod(y - d, NY)], S_AC + d)

    def rows_of(q, arr):
        lo = arr * 128
        return jnp.concatenate([a[q % 2, (q // 2) * 2 + p, lo : lo + 128, :] for p in range(2)], axis=0)

    db_q = [rows_of(q, 1) for q in range(4)]
    with jax.named_scope("ring_e"):
        landed(g.at[mod(z - 8, NZ)], S_RR + 7)
        put(mod(z - 8, NZ))

    with jax.named_scope("project"):

        def w_of(q, lo, hi):
            return wp[4 * q : 4 * q + 4, :, lo:hi].reshape(FPAD, hi - lo)

        raw = dot(rows_of(0, 0), w_of(0, 0, 768))
        d_att = dot(db_q[0], w_of(0, 768, 1024))
        for q in range(1, 4):
            raw += dot(rows_of(q, 0), w_of(q, 0, 768))
            d_att += dot(db_q[q], w_of(q, 768, 1024))
        d_att = d_att.astype(BF)

    q_gain, k_gain = qg_ref[...], kg_ref[...]
    factor = 1.0 / np.sqrt(np.float32(HD))
    row_i = lax.broadcasted_iota(jnp.int32, (128, 128), 0) % 2
    col_i = lax.broadcasted_iota(jnp.int32, (128, 128), 1) % 2
    same = row_i == col_i

    def norm(v, gain):
        root = lax.rsqrt(jnp.sum(v * v, axis=-1, keepdims=True) * (1.0 / HD) + 1e-06)
        return (v * root * gain).astype(BF), root

    with jax.named_scope("attend"):
        state = []
        att = []
        for p in range(2):
            for h in range(2):
                rows = slice(128 * p, 128 * p + 128)
                rq, rk = raw[rows, 128 * h : 128 * h + 128], raw[rows, 256 + 128 * h : 384 + 128 * h]
                v = raw[rows, 512 + 128 * h : 640 + 128 * h].astype(BF)
                qn, root_q = norm(rq, q_gain)
                kn, root_k = norm(rk, k_gain)
                s = jnp.where(same, dot_nt(qn, kn) * factor, -1e30)
                e = jnp.exp(s - jnp.max(s, axis=-1, keepdims=True))
                pr = e / jnp.sum(e, axis=-1, keepdims=True)
                pb = pr.astype(BF)
                att.append(dot(pb, v).astype(BF))
                state.append((rq, rk, v, qn, kn, root_q, root_k, pr, pb))
        att = jnp.concatenate(
            [jnp.concatenate([att[0], att[1]], axis=1), jnp.concatenate([att[2], att[3]], axis=1)], axis=0
        )

    def spread(q, val, buf):
        for p in range(2):
            buf[q % 2, (q // 2) * 2 + p] = val[128 * p : 128 * p + 128].astype(BF)

    with jax.named_scope("branch"):
        for q in range(4):
            spread(q, dot_nt(att, w_of(q, 768, 1024)), bp)
        send(bp.at[1 - core], bq, S_B, across)

    with jax.named_scope("proj_grad"):
        att_c = jnp.concatenate(
            [dot(att[:128], p_h0[...]).astype(BF), dot(att[128:], p_h1[...]).astype(BF)], axis=0
        )
        for q in range(4):
            dbx = dot(db_q[q], p_pg[...]).astype(BF)
            px[:, 80 * q : 80 * q + 80] = dot_tn(dbx, att_c).astype(BF).reshape(NX, 80, 288)
        for d in range(1, NX):
            to = mod(x + d, NX)
            send(px.at[to], pxr.at[d - 1], S_PX + d - 1, at_x(d))

    with jax.named_scope("attend_back"):
        d_raw = [[], []]
        for p in range(2):
            cols_q, cols_k, cols_v = [], [], []
            for h in range(2):
                rq, rk, v, qn, kn, root_q, root_k, pr, pb = state[2 * p + h]
                da = d_att[128 * p : 128 * p + 128, 128 * h : 128 * h + 128]
                dv = dot_tn(pb, da).astype(BF)
                d_p = dot_nt(da, v)
                ds = (pr * (d_p - jnp.sum(pr * d_p, axis=-1, keepdims=True)) * factor).astype(BF)
                dq = dot(ds, kn).astype(BF)
                dk = dot_tn(ds, qn).astype(BF)

                def norm_back(v_raw, root, gain, d_n):
                    gq = gain * d_n.astype(F32)
                    inner = jnp.sum(v_raw * gq, axis=-1, keepdims=True) * (1.0 / HD)
                    return (root * gq - v_raw * (root * root * root) * inner).astype(BF)

                cols_q.append(norm_back(rq, root_q, q_gain, dq))
                cols_k.append(norm_back(rk, root_k, k_gain, dk))
                cols_v.append(dv)
            d_raw[p] = jnp.concatenate(cols_q + cols_k + cols_v, axis=1)
        d_raw = jnp.concatenate(d_raw, axis=0)
        for q in range(4):
            spread(q, dot_nt(d_raw, w_of(q, 0, 768)), hp)
        send(hp.at[1 - core], hq, S_H, across)

    def to_y(own, got, total, far, base):
        landed(got, base)
        total[...] = (own[core].astype(F32) + got[...].astype(F32)).astype(BF)
        for d in range(1, NY):
            send(total.at[mod(y + d, NY)], far.at[d - 1], base + d, at_y(d))

    def y_sum(total, far, base):
        for d in range(1, NY):
            landed(far.at[d - 1], base + d)
        s = total[y].astype(F32)
        for d in range(1, NY):
            s += far[d - 1].astype(F32)
        return s

    with jax.named_scope("branch_y"):
        to_y(bp, bq, bt, bu, S_B)
    with jax.named_scope("hidden_y"):
        to_y(hp, hq, ht, hu, S_H)
    with jax.named_scope("grad_x"):
        for d in range(1, NX):
            landed(pxr.at[d - 1], S_PX + d - 1)
        s = px[x].astype(F32)
        for d in range(1, NX):
            s += pxr[d - 1].astype(F32)
        s = s.astype(BF)
        for q in range(4):
            pz[4 * q : 4 * q + 4] = dot(p_pz[...], s[80 * q : 80 * q + 80]).astype(BF).reshape(4, 32, 288)
        z_send(pz, pzr, S_PZ)
        pzr[z] = pz[z]
    with jax.named_scope("back_z"):
        branch = y_sum(bt, bu, S_B)
        hidden = y_sum(ht, hu, S_H)
        both = jnp.concatenate([branch.reshape(NZ, 8, FPAD), hidden.reshape(NZ, 8, FPAD)], axis=1)
        zb[...] = both.astype(BF)
        z_send(zb, r3, S_Z2)
        r3[z] = zb[z]
        z_landed(r3, S_Z2)
    with jax.named_scope("back_x"):
        xs[...] = dot(p_z2[...], r3[...].reshape(256, FPAD)).astype(BF).reshape(NX, 64, FPAD)
        for d in range(1, NX):
            send(xs.at[mod(x + d, NX)], r4.at[x], S_X2 + d - 1, at_x(d))
        r4[x] = xs[x]
        for d in range(1, NX):
            landed(r4.at[mod(x - d, NX)], S_X2 + d - 1)
        own = dot(p_x2[...], r4[...].reshape(256, FPAD)).astype(BF)
        oa[hd] = dot(own, unpad[...]).astype(BF)
    with jax.named_scope("back_head"):
        far_hd = mod(hd + 2, 4)
        send(oa.at[hd], oa.at[hd], S_OY, at_y(2))
        send(oa.at[hd], oa.at[hd], S_OC, across)
    with jax.named_scope("grad_z"):
        z_landed(pzr, S_PZ)
        s = pzr[0].astype(F32)
        for k in range(1, NZ):
            s += pzr[k].astype(F32)
        pgs[dp] = s
        send(pgs.at[dp], pgs.at[dp], S_PY, at_y(1 - 2 * dp))
    with jax.named_scope("back_core"):
        landed(oa.at[far_hd], S_OY)
        send(oa.at[far_hd], oa.at[far_hd], S_OC + 1, across)
        landed(oa.at[hd + 1 - 2 * core], S_OC)
        landed(oa.at[mod(hd + 3 - 2 * core, 4)], S_OC + 1)
        out_ref[...] = oa[...]
        landed(pgs.at[1 - dp], S_PY)
        pg_ref[...] = pgs[...]

    with jax.named_scope("sent"):
        for c in sends:
            c.wait_send()

        def ring_sent(s, c):
            right(s).wait_send()
            left(s).wait_send()
            return c

        lax.fori_loop(1, 8, ring_sent, 0)
        right(8).wait_send()
        z_sent(z1, r2, S_Z1)
        z_sent(zb, r3, S_Z2)
        z_sent(pz, pzr, S_PZ)


def per_device(inputs, modulation, qkv_weight, proj_weight, q_gain, k_gain, cotangent):
    _, spatial_n, width = inputs.shape
    hd, dp = lax.axis_index("head"), lax.axis_index("dp")
    inputs_f = inputs[0].astype(F32)
    shift_vec, scale_vec, gate_vec = (modulation[0], modulation[1], modulation[2])
    center = jnp.mean(inputs_f, axis=1, keepdims=True)
    centered = inputs_f - center
    rstd_col = 1.0 / jnp.sqrt(jnp.mean(centered * centered, axis=1, keepdims=True) + 1e-06)
    normed = centered * rstd_col
    hidden_in = (normed * (1.0 + scale_vec) + shift_vec).astype(BF)
    d_out = cotangent[0].astype(F32)
    d_branch = (gate_vec * d_out).astype(BF)

    both = jnp.stack([hidden_in, d_branch])
    both = lax.dynamic_slice_in_dim(both, hd * 288, 288, axis=2)
    both = both.reshape(2, NZ, NX, 2, 4, HD).transpose(2, 1, 0, 3, 4, 5)
    both = jnp.pad(both, [(0, 0)] * 5 + [(0, 8)]).reshape(NX, 64, FPAD)

    w_half = lax.dynamic_slice_in_dim(qkv_weight, dp * 144, 144, axis=2)
    w_half = w_half.transpose(1, 0, 2).reshape(18, 432)
    p_half = lax.dynamic_slice_in_dim(proj_weight, dp * 144, 144, axis=0).T
    w_in = jnp.pad(jnp.concatenate([w_half, p_half], axis=1), [(0, 14), (0, 0)])

    gains = [jnp.pad(v, (0, 56)).reshape(1, 128) for v in (q_gain, k_gain)]
    consts = [jnp.asarray(m) for m in selections()]

    def vm(*shape, dtype=BF):
        return pltpu.VMEM(shape, dtype)

    out, pg = pl.pallas_call(
        kernel,
        out_shape=(
            jax.ShapeDtypeStruct((4, 256, 288), BF),
            jax.ShapeDtypeStruct((2, 32, 288), F32),
        ),
        in_specs=[pl.BlockSpec(memory_space=pltpu.VMEM)] * (4 + len(consts)),
        out_specs=[pl.BlockSpec(memory_space=pltpu.VMEM)] * 2,
        scratch_shapes=[
            vm(NX, 32, WCOLS),
            vm(NZ, 80, WCOLS),
            vm(NZ, 80, 1024),
            vm(NX, 64, FPAD),
            vm(NZ, 16, FPAD),
            vm(NZ, 16, FPAD),
            vm(2, NY, 256, FPAD),
            vm(2, NY, 128, FPAD),
            vm(NY, 128, FPAD),
            vm(NY, 128, FPAD),
            vm(3, 128, FPAD),
            vm(2, NY, 128, FPAD),
            vm(NY, 128, FPAD),
            vm(NY, 128, FPAD),
            vm(3, 128, FPAD),
            vm(NZ, 16, FPAD),
            vm(NZ, 16, FPAD),
            vm(NX, 64, FPAD),
            vm(NX, 64, FPAD),
            vm(4, 256, 288),
            vm(NX, 320, 288),
            vm(3, 320, 288),
            vm(NZ, 32, 288),
            vm(NZ, 32, 288),
            vm(2, 32, 288, dtype=F32),
            pltpu.SemaphoreType.DMA((N_SEM,)),
            pltpu.SemaphoreType.DMA((N_SEM,)),
        ],
        compiler_params=pltpu.CompilerParams(
            collective_id=0, has_side_effects=True, vmem_limit_bytes=48 * 1024 * 1024
        ),
    )(w_in, both, *gains, *consts)

    out = out.reshape(4, 2, spatial_n, 288).transpose(1, 2, 0, 3).reshape(2, spatial_n, width)
    branch, d_hidden = out[0].astype(F32), out[1].astype(F32)
    output = (inputs_f + gate_vec * branch).astype(BF)
    d_normed = d_hidden * (1.0 + scale_vec)
    d_in = rstd_col * (
        d_normed
        - jnp.mean(d_normed, axis=1, keepdims=True)
        - normed * jnp.mean(d_normed * normed, axis=1, keepdims=True)
    )
    input_grad = (d_out + d_in).astype(BF)
    pg = lax.dynamic_slice(pg, (0, 0, dp * 144), (2, 18, 144))
    proj_grad = pg.transpose(0, 2, 1).reshape(288, 18)
    return output[None], input_grad[None], proj_grad


def solution(mesh):
    return jax.shard_map(
        per_device,
        mesh=mesh,
        in_specs=(
            P(("dp", "frame"), None, None),
            P("dp", None),
            P(None, "frame", "head"),
            P("head", "frame"),
            P(),
            P(),
            P(("dp", "frame"), None, None),
        ),
        out_specs=(
            P(("dp", "frame"), None, None),
            P(("dp", "frame"), None, None),
            P(("dp", "head"), "frame"),
        ),
        check_vma=False,
    )
```

```python
import jax
import jax.numpy as jnp
import numpy as np
from jax import lax
from jax.experimental import pallas as pl
from jax.experimental.pallas import tpu as pltpu
from jax.sharding import PartitionSpec as P

MESH = pl.DeviceIdType.MESH
BF = jnp.bfloat16
F32 = jnp.float32
NZ, NX, NY = 16, 4, 4
HD = 72
QF = 288
QKV, WCOLS = 432, 576

S_X1 = 0
S_WZ = S_X1 + 3
S_Z1 = S_WZ + 15
S_WX = S_Z1 + 15
S_AY = S_WX + 3
S_AC = S_AY + 3
S_B = S_AC + 4
S_H = S_B + 4
S_Z2 = S_H + 4
S_X2 = S_Z2 + 15
S_XF = S_X2 + 3
S_OC = S_XF + 4
S_PX = S_OC + 2
S_PZ = S_PX + 3
S_PY = S_PZ + 15
N_SEM = S_PY + 1


def one_hot(shape, pairs):
    m = np.zeros(shape, np.float32)
    for r, c in pairs:
        m[r, c] = 1.0
    return m.astype(jnp.bfloat16)


def selections():
    r2, r4, r16 = range(2), range(4), range(16)
    rows = [(a, z, x, i) for a in r2 for z in r16 for x in r4 for i in r2]
    return [
        one_hot((256, 256), [(x * 64 + z * 4 + a * 2 + i, a * 128 + z * 8 + x * 2 + i) for a, z, x, i in rows]),
        one_hot((256, 256), [(z * 16 + a * 8 + x * 2 + i, x * 64 + z * 4 + a * 2 + i) for a, z, x, i in rows]),
        one_hot((256, 256), [(a * 128 + z * 8 + x * 2 + i, z * 16 + a * 8 + x * 2 + i) for a, z, x, i in rows]),
        one_hot((256, 256), [(x * 64 + a * 32 + z * 2 + i, z * 16 + a * 8 + x * 2 + i) for a, z, x, i in rows]),
        one_hot((256, 256), [(a * 128 + z * 8 + x * 2 + i, x * 64 + a * 32 + z * 2 + i) for a, z, x, i in rows]),
        one_hot((72, WCOLS), [(j, g * 72 + j) for g in range(8) for j in range(72)]),
        one_hot((32, 256), [(r, 8 * r + k) for r in range(32) for k in range(8)]),
        one_hot((256, 32), [(z * 16 + o * 4 + k, z * 2 + o) for z in r16 for o in r2 for k in r4]),
    ]


def dot(a, b):
    return jnp.dot(a, b, preferred_element_type=F32)


def dot_nt(a, b):
    return lax.dot_general(a, b, (((1,), (1,)), ((), ())), preferred_element_type=F32)


def dot_tn(a, b):
    return lax.dot_general(a, b, (((0,), (0,)), ((), ())), preferred_element_type=F32)


def mod(a, n):
    return lax.rem(a + n, n)


def kernel(
    w_in, in_ref, cot_ref, mod_ref, qg_ref, kg_ref, p_x0, p_x1, p_z1, p_z2, p_x2, repeat, sum8, widen,
    out_ref, ig_ref, pg_ref,
    order, rows_in, r1, wz, z1, r2, xw, a, bp, bq, bt, bu, hp, hq, ht, hu, zb, r3, xs, r4, px, pxr, pz, pzr, pgs,
    ss, rs,
):
    f, hd, dp = lax.axis_index("frame"), lax.axis_index("head"), lax.axis_index("dp")
    z, x = f // NX, lax.rem(f, NX)
    core, y = lax.rem(hd, 2), (hd // 2) * 2 + dp
    far_hd = mod(hd + 2, 4)

    def at_x(d):
        return (z * NX + mod(x + d, NX), hd, dp)

    def at_x_far(d):
        return (z * NX + mod(x + d, NX), far_hd, dp)

    def at_z(d):
        return (mod(z + d, NZ) * NX + x, hd, dp)

    def at_y(d):
        yy = mod(y + d, NY)
        return (f, (yy // 2) * 2 + core, lax.rem(yy, 2))

    across = (f, hd + 1 - 2 * core, dp)

    def copy(src, dst, i, dev):
        return pltpu.make_async_remote_copy(
            src_ref=src, dst_ref=dst, send_sem=ss.at[i], recv_sem=rs.at[i], device_id=dev, device_id_type=MESH
        )

    sent = []

    def send(*args):
        c = copy(*args)
        c.start()
        sent.append(c.wait_send)

    def landed(ref, i):
        copy(ref, ref, i, across).wait_recv()

    def z_send(src_of, dst, base):
        def each(d, c):
            copy(src_of(mod(z + d, NZ)), dst.at[z], base + d - 1, at_z(d)).start()
            return c

        lax.fori_loop(1, NZ, each, 0)

        def each_sent(d, c):
            copy(src_of(mod(z + d, NZ)), dst.at[z], base + d - 1, at_z(d)).wait_send()
            return c

        sent.append(lambda: lax.fori_loop(1, NZ, each_sent, 0))

    def z_landed(dst, base):
        def each(d, c):
            landed(dst.at[mod(z - d, NZ)], base + d - 1)
            return c

        lax.fori_loop(1, NZ, each, 0)

    barrier = pltpu.get_barrier_semaphore()

    def greet(dev):
        pl.semaphore_signal(barrier, inc=1, device_id=dev, device_id_type=MESH)

    with jax.named_scope("greet"):

        def greet_z(d, c):
            greet(at_z(d))
            return c

        lax.fori_loop(1, NZ, greet_z, 0)
        for d in range(1, NX):
            greet(at_x(d))
            greet(at_x_far(d))
        for d in range(1, NY):
            greet(at_y(d))
        greet(across)

    def mean(v):
        return jnp.sum(v, axis=1, keepdims=True) * (1.0 / v.shape[1])

    def normalise():
        v = in_ref[...].astype(F32)
        v = v - mean(v)
        root = lax.rsqrt(mean(v * v) + 1e-06)
        return v * root, root

    with jax.named_scope("rows"):
        feature = lax.broadcasted_iota(jnp.int32, (1152, QF), 0)
        col = lax.broadcasted_iota(jnp.int32, (1, QF), 1)
        last = col - 256
        from_col = jnp.where(col < 256, (col // 16) * 72 + col % 16, (last // 2) * 72 + 16 + last % 2)
        for q in range(4):
            order[q] = jnp.where(feature == from_col + 18 * q, 1.0, 0.0).astype(BF)
        normed, _ = normalise()
        hidden_in = (normed * (1.0 + mod_ref[1:2]) + mod_ref[0:1]).astype(BF)
        d_branch = (mod_ref[2:3] * cot_ref[...].astype(F32)).astype(BF)
        quarter = dot(jnp.concatenate([hidden_in, d_branch], axis=0), order[hd]).astype(BF)
        rows_in[...] = dot(p_x0[...], quarter).astype(BF).reshape(NX, 64, QF)

    with jax.named_scope("greeted"):
        pl.semaphore_wait(barrier, 25)

    with jax.named_scope("rows_x"):
        for d in range(1, NX):
            send(rows_in.at[mod(x + d, NX)], r1.at[x], S_X1 + d - 1, at_x(d))
        z_send(lambda k: w_in, wz, S_WZ)
        r1[x] = rows_in[x]
        wz[z] = w_in[...]
        for d in range(1, NX):
            landed(r1.at[mod(x - d, NX)], S_X1 + d - 1)
        z1[...] = dot(p_x1[...], r1[...].reshape(256, QF)).astype(BF).reshape(NZ, 16, QF)
        z_send(lambda k: z1.at[k], r2, S_Z1)
        r2[z] = z1[z]

    with jax.named_scope("weights_z"):
        z_landed(wz, S_WZ)
        xw[x, 0:256] = wz[:, :, 0:WCOLS].reshape(256, WCOLS)
        tail = dot(wz[:, :, WCOLS : WCOLS + 72].reshape(256, 72), repeat[...])
        row8 = lax.broadcasted_iota(jnp.int32, (256, WCOLS), 0) % 8
        group = lax.broadcasted_iota(jnp.int32, (1, WCOLS), 1) // 72
        tail = jnp.where(row8 == group, tail, 0.0).astype(BF)
        xw[x, 256:288] = dot(sum8[...], tail).astype(BF)
        for d in (2, 1, 3):
            send(xw.at[x], xw.at[x], S_WX + d - 1, at_x(d))

    with jax.named_scope("rows_z"):
        z_landed(r2, S_Z1)
        a[core, y] = dot(p_z1[...], r2[...].reshape(256, QF)).astype(BF)
        for d in (2, 1, 3):
            send(a.at[core, y], a.at[core, y], S_AY + d - 1, at_y(d))
        send(a.at[core, y], a.at[core, y], S_AC, across)

    with jax.named_scope("rows_y"):
        for d in (1, 3, 2):
            slot = a.at[core, mod(y - d, NY)]
            landed(slot, S_AY + d - 1)
            send(slot, slot, S_AC + d, across)
        for d in range(NY):
            landed(a.at[1 - core, mod(y - d, NY)], S_AC + d)

    def rows_of(q, arr):
        lo = arr * 128
        return jnp.concatenate([a[q % 2, (q // 2) * 2 + p, lo : lo + 128, :] for p in range(2)], axis=0)

    with jax.named_scope("project"):

        def project(q):
            w = xw[q]
            return dot(rows_of(q, 0), w[:, :QKV]), dot(rows_of(q, 1), w[:, QKV:])

        raw, d_att = project(x)
        for d in (1, 3, 2):
            q = mod(x - d, NX)
            landed(xw.at[q], S_WX + d - 1)
            more_raw, more_d = project(q)
            raw, d_att = raw + more_raw, d_att + more_d
        d_att = d_att.astype(BF)

    q_gain, k_gain = qg_ref[...], kg_ref[...]
    factor = 1.0 / np.sqrt(np.float32(HD))
    row_i = lax.broadcasted_iota(jnp.int32, (128, 128), 0) % 2
    col_i = lax.broadcasted_iota(jnp.int32, (128, 128), 1) % 2
    same = row_i == col_i

    def norm(v, gain):
        root = lax.rsqrt(jnp.sum(v * v, axis=-1, keepdims=True) * (1.0 / HD) + 1e-06)
        return (v * root * gain).astype(BF), root

    def part_cols(v, p, k):
        return v[128 * p : 128 * p + 128, HD * k : HD * k + HD]

    with jax.named_scope("attend"):
        state, att = [], [[], []]
        for p in range(2):
            for h in range(2):
                rq, rk, v = (part_cols(raw, p, 2 * w + h) for w in range(3))
                v = v.astype(BF)
                qn, root_q = norm(rq, q_gain)
                kn, root_k = norm(rk, k_gain)
                s = jnp.where(same, dot_nt(qn, kn) * factor, -1e30)
                e = jnp.exp(s - jnp.max(s, axis=-1, keepdims=True))
                pr = e / jnp.sum(e, axis=-1, keepdims=True)
                pb = pr.astype(BF)
                att[p].append(dot(pb, v).astype(BF))
                state.append((rq, rk, v, qn, kn, root_q, root_k, pr, pb))
        att = [jnp.concatenate(half, axis=1) for half in att]

    def spread(q, val, buf):
        for p in range(2):
            buf[q % 2, (q // 2) * 2 + p] = val[128 * p : 128 * p + 128].astype(BF)

    with jax.named_scope("branch"):
        both = jnp.concatenate(att, axis=0)
        for q in range(4):
            spread(q, dot_nt(both, xw[q, :, QKV:]), bp)
        send(bp.at[1 - core], bq, S_B, across)

    with jax.named_scope("attend_back"):
        d_raw = []
        for p in range(2):
            cols_q, cols_k, cols_v = [], [], []
            for h in range(2):
                rq, rk, v, qn, kn, root_q, root_k, pr, pb = state[2 * p + h]
                da = part_cols(d_att, p, h)
                dv = dot_tn(pb, da).astype(BF)
                d_p = dot_nt(da, v)
                ds = (pr * (d_p - jnp.sum(pr * d_p, axis=-1, keepdims=True)) * factor).astype(BF)
                dq = dot(ds, kn).astype(BF)
                dk = dot_tn(ds, qn).astype(BF)

                def norm_back(v_raw, root, gain, d_n):
                    gq = gain * d_n.astype(F32)
                    inner = jnp.sum(v_raw * gq, axis=-1, keepdims=True) * (1.0 / HD)
                    return (root * gq - v_raw * (root * root * root) * inner).astype(BF)

                cols_q.append(norm_back(rq, root_q, q_gain, dq))
                cols_k.append(norm_back(rk, root_k, k_gain, dk))
                cols_v.append(dv)
            d_raw.append(jnp.concatenate(cols_q + cols_k + cols_v, axis=1))
        d_raw = jnp.concatenate(d_raw, axis=0)
        for q in range(4):
            spread(q, dot_nt(d_raw, xw[q, :, :QKV]), hp)
        send(hp.at[1 - core], hq, S_H, across)

    def to_y(own, got, total, far, base):
        landed(got, base)
        total[...] = (own[core].astype(F32) + got[...].astype(F32)).astype(BF)
        for d in (2, 1, 3):
            send(total.at[mod(y + d, NY)], far.at[d - 1], base + d, at_y(d))

    def y_sum(total, far, base):
        for d in range(1, NY):
            landed(far.at[d - 1], base + d)
        s = total[y].astype(F32)
        for d in range(1, NY):
            s += far[d - 1].astype(F32)
        return s

    with jax.named_scope("branch_y"):
        to_y(bp, bq, bt, bu, S_B)
    with jax.named_scope("hidden_y"):
        to_y(hp, hq, ht, hu, S_H)

    with jax.named_scope("proj_grad"):
        none = jnp.zeros((128, 144), BF)
        att_c = jnp.concatenate(
            [jnp.concatenate([att[0], none], axis=1), jnp.concatenate([none, att[1]], axis=1)], axis=0
        )
        for q in range(4):
            px[q] = dot_tn(rows_of(q, 1), att_c).astype(BF)
        for d in (2, 1, 3):
            send(px.at[mod(x + d, NX)], pxr.at[d - 1], S_PX + d - 1, at_x(d))

    with jax.named_scope("back_z"):
        branch = y_sum(bt, bu, S_B)
        hidden = y_sum(ht, hu, S_H)
        pair = jnp.concatenate([branch.reshape(NZ, 8, QF), hidden.reshape(NZ, 8, QF)], axis=1)
        zb[...] = pair.astype(BF)
        z_send(lambda k: zb.at[k], r3, S_Z2)
        r3[z] = zb[z]

    with jax.named_scope("grad_x"):
        for d in range(1, NX):
            landed(pxr.at[d - 1], S_PX + d - 1)
        s = px[x].astype(F32)
        for d in range(1, NX):
            s += pxr[d - 1].astype(F32)
        tail = dot(widen[...], s[256:288].astype(BF))
        row4 = lax.broadcasted_iota(jnp.int32, (256, QF), 0) % 4
        group = lax.broadcasted_iota(jnp.int32, (1, QF), 1) // 72
        tail = jnp.where(row4 == group, tail, 0.0)
        tail = tail[:, 0:72] + tail[:, 72:144] + tail[:, 144:216] + tail[:, 216:288]
        pz[...] = jnp.concatenate([s[0:256], tail], axis=1).astype(BF).reshape(NZ, 16, 360)
        z_send(lambda k: pz.at[k], pzr, S_PZ)
        pzr[z] = pz[z]

    with jax.named_scope("back_x"):
        z_landed(r3, S_Z2)
        xs[...] = dot(p_z2[...], r3[...].reshape(256, QF)).astype(BF).reshape(NX, 64, QF)
        for d in (2, 1, 3):
            to = mod(x + d, NX)
            send(xs.at[to], r4.at[hd, x], S_XF + d, at_x_far(d))
            send(xs.at[to], r4.at[hd, x], S_X2 + d - 1, at_x(d))
        send(xs.at[x], r4.at[hd, x], S_XF, at_y(2))
        r4[hd, x] = xs[x]
        for d in range(1, NX):
            landed(r4.at[hd, mod(x - d, NX)], S_X2 + d - 1)
        send(r4.at[hd], r4.at[hd], S_OC, across)
        for d in range(NX):
            landed(r4.at[far_hd, mod(x - d, NX)], S_XF + d)
        send(r4.at[far_hd], r4.at[far_hd], S_OC + 1, across)

    with jax.named_scope("grad_z"):
        z_landed(pzr, S_PZ)
        s = pzr[0].astype(F32)
        for k in range(1, NZ):
            s += pzr[k].astype(F32)
        pgs[dp] = s
        send(pgs.at[dp], pgs.at[dp], S_PY, at_y(1 - 2 * dp))

    with jax.named_scope("results"):

        def natural(q):
            return dot_nt(dot(p_x2[...], r4[q].reshape(256, QF)).astype(BF), order[q])

        total = natural(hd) + natural(far_hd)
        landed(r4.at[hd + 1 - 2 * core], S_OC)
        total += natural(hd + 1 - 2 * core)
        landed(r4.at[mod(hd + 3 - 2 * core, 4)], S_OC + 1)
        total += natural(mod(hd + 3 - 2 * core, 4))
        out_ref[...] = (in_ref[...].astype(F32) + mod_ref[2:3] * total[0:128]).astype(BF)
        normed, root = normalise()
        d_n = total[128:256] * (1.0 + mod_ref[1:2])
        d_in = root * (d_n - mean(d_n) - normed * mean(d_n * normed))
        ig_ref[...] = (cot_ref[...].astype(F32) + d_in).astype(BF)
        landed(pgs.at[1 - dp], S_PY)
        pg_ref[...] = pgs[...]

    with jax.named_scope("sent"):
        for wait in sent:
            wait()


def per_device(inputs, modulation, qkv_weight, proj_weight, q_gain, k_gain, cotangent):
    dp = lax.axis_index("dp")
    tokens, width = inputs.shape[1:]

    w_half = lax.dynamic_slice_in_dim(qkv_weight, dp * 144, 144, axis=2)
    w_half = w_half.transpose(1, 0, 2).reshape(18, QKV)
    p_half = lax.dynamic_slice_in_dim(proj_weight, dp * 144, 144, axis=0).T
    w_all = jnp.concatenate([w_half, p_half], axis=1)
    w_in = jnp.concatenate([w_all[:16], w_all[16:].reshape(16, HD)], axis=1)

    consts = [jnp.asarray(m) for m in selections()]

    def vm(*shape, dtype=BF):
        return pltpu.VMEM(shape, dtype)

    out, ig, pg = pl.pallas_call(
        kernel,
        out_shape=(
            jax.ShapeDtypeStruct((tokens, width), BF),
            jax.ShapeDtypeStruct((tokens, width), BF),
            jax.ShapeDtypeStruct((2, 16, 360), F32),
        ),
        in_specs=[pl.BlockSpec(memory_space=pltpu.VMEM)] * (6 + len(consts)),
        out_specs=[pl.BlockSpec(memory_space=pltpu.VMEM)] * 3,
        scratch_shapes=[
            vm(4, 1152, QF),
            vm(NX, 64, QF),
            vm(NX, 64, QF),
            vm(NZ, 16, WCOLS + HD),
            vm(NZ, 16, QF),
            vm(NZ, 16, QF),
            vm(NX, QF, WCOLS),
            vm(2, NY, 256, QF),
            vm(2, NY, 128, QF),
            vm(NY, 128, QF),
            vm(NY, 128, QF),
            vm(3, 128, QF),
            vm(2, NY, 128, QF),
            vm(NY, 128, QF),
            vm(NY, 128, QF),
            vm(3, 128, QF),
            vm(NZ, 16, QF),
            vm(NZ, 16, QF),
            vm(NX, 64, QF),
            vm(4, NX, 64, QF),
            vm(NX, QF, QF),
            vm(3, QF, QF),
            vm(NZ, 16, 360),
            vm(NZ, 16, 360),
            vm(2, 16, 360, dtype=F32),
            pltpu.SemaphoreType.DMA((N_SEM,)),
            pltpu.SemaphoreType.DMA((N_SEM,)),
        ],
        compiler_params=pltpu.CompilerParams(
            collective_id=0, has_side_effects=True, vmem_limit_bytes=48 * 1024 * 1024
        ),
    )(w_in, inputs[0], cotangent[0], modulation, q_gain[None], k_gain[None], *consts)

    pg = jnp.concatenate([pg[:, :, :QF], pg[:, :8, QF:].reshape(2, 2, QF)], axis=1)
    pg = lax.dynamic_slice(pg, (0, 0, dp * 144), (2, 18, 144))
    proj_grad = pg.transpose(0, 2, 1).reshape(288, 18)
    return out[None], ig[None], proj_grad


def solution(mesh):
    return jax.shard_map(
        per_device,
        mesh=mesh,
        in_specs=(
            P(("dp", "frame"), None, None),
            P("dp", None),
            P(None, "frame", "head"),
            P("head", "frame"),
            P(),
            P(),
            P(("dp", "frame"), None, None),
        ),
        out_specs=(
            P(("dp", "frame"), None, None),
            P(("dp", "frame"), None, None),
            P(("dp", "head"), "frame"),
        ),
        check_vma=False,
    )
```

```python
import jax
import jax.numpy as jnp
import numpy as np
from jax import lax
from jax.experimental import pallas as pl
from jax.experimental.pallas import tpu as pltpu
from jax.sharding import PartitionSpec as P

MESH = pl.DeviceIdType.MESH
BF = jnp.bfloat16
F32 = jnp.float32
NZ, NX, NY = 16, 4, 4
HD = 72
GF = 80
QF = 4 * GF
QKV, WCOLS = 432, 576

S_Z1 = 0
S_X1 = S_Z1 + 15
S_W4 = S_X1 + 3
S_WX = S_W4 + 3
S_AY = S_WX + 16
S_AC = S_AY + 3
S_B = S_AC + 4
S_H = S_B + 4
S_Z2 = S_H + 4
S_X2 = S_Z2 + 15
S_XF = S_X2 + 3
S_OC = S_XF + 4
S_PX = S_OC + 2
S_PZ = S_PX + 3
S_PY = S_PZ + 15
N_SEM = S_PY + 1


def pick(rows, cols, source):
    r = lax.broadcasted_iota(jnp.int32, (rows, 1), 0)
    c = lax.broadcasted_iota(jnp.int32, (rows, cols), 1)
    return jnp.where(c == source(r), 1.0, 0.0).astype(BF)


def dot(a, b):
    return jnp.dot(a, b, preferred_element_type=F32)


def dot_nt(a, b):
    return lax.dot_general(a, b, (((1,), (1,)), ((), ())), preferred_element_type=F32)


def dot_tn(a, b):
    return lax.dot_general(a, b, (((0,), (0,)), ((), ())), preferred_element_type=F32)


def mod(a, n):
    return lax.rem(a + n, n)


def kernel(
    in_hbm, cot_hbm, mod_hbm, qkv_hbm, proj_hbm, qg_hbm, kg_hbm,
    out_ref, ig_ref, pg_ref,
    in_ref, cot_ref, mod_ref, qkv_ref, proj_ref, qg_ref, kg_ref,
    order, perm, w_in, rows_in, r1, w4, z1, r2, xw, a, bp, bq, bt, bu, hp, hq, ht, hu, zb, r3, xs, r4, px, pxr, pz, pzr, pgs,
    ss, rs, ls,
):
    fetches = [
        pltpu.make_async_copy(src, dst, ls.at[i])
        for i, (src, dst) in enumerate(
            [
                (qkv_hbm, qkv_ref), (proj_hbm, proj_ref), (in_hbm, in_ref), (cot_hbm, cot_ref),
                (mod_hbm, mod_ref), (qg_hbm, qg_ref), (kg_hbm, kg_ref),
            ]
        )
    ]
    for fetch in fetches:
        fetch.start()

    f, hd, dp = lax.axis_index("frame"), lax.axis_index("head"), lax.axis_index("dp")
    z, x = f // NX, lax.rem(f, NX)
    core, y = lax.rem(hd, 2), (hd // 2) * 2 + dp
    far_hd = mod(hd + 2, 4)

    def at_x(d):
        return (z * NX + mod(x + d, NX), hd, dp)

    def at_x_far(d):
        return (z * NX + mod(x + d, NX), far_hd, dp)

    def at_zx(dz, dx):
        return (mod(z + dz, NZ) * NX + mod(x + dx, NX), hd, dp)

    def at_z(d):
        return (mod(z + d, NZ) * NX + x, hd, dp)

    def at_y(d):
        yy = mod(y + d, NY)
        return (f, (yy // 2) * 2 + core, lax.rem(yy, 2))

    across = (f, hd + 1 - 2 * core, dp)

    def copy(src, dst, i, dev):
        return pltpu.make_async_remote_copy(
            src_ref=src, dst_ref=dst, send_sem=ss.at[i], recv_sem=rs.at[i], device_id=dev, device_id_type=MESH
        )

    sent = []

    def send(*args):
        c = copy(*args)
        c.start()
        sent.append(c.wait_send)

    def landed(ref, i):
        copy(ref, ref, i, across).wait_recv()

    def z_send(src_of, dst, base):
        def each(d, c):
            copy(src_of(mod(z + d, NZ)), dst.at[z], base + d - 1, at_z(d)).start()
            return c

        lax.fori_loop(1, NZ, each, 0)

        def each_sent(d, c):
            copy(src_of(mod(z + d, NZ)), dst.at[z], base + d - 1, at_z(d)).wait_send()
            return c

        sent.append(lambda: lax.fori_loop(1, NZ, each_sent, 0))

    def z_landed(dst, base):
        def each(d, c):
            landed(dst.at[mod(z - d, NZ)], base + d - 1)
            return c

        lax.fori_loop(1, NZ, each, 0)

    barrier = pltpu.get_barrier_semaphore()

    def greet(dev):
        pl.semaphore_signal(barrier, inc=1, device_id=dev, device_id_type=MESH)

    with jax.named_scope("greet"):

        def greet_z(d, c):
            greet(at_z(d))
            return c

        lax.fori_loop(1, NZ, greet_z, 0)
        for d in range(1, NX):
            greet(at_x(d))
            greet(at_x_far(d))
            for dz in (-2, -1, 1, 2):
                greet(at_zx(dz, d))
        for d in range(1, NY):
            greet(at_y(d))
        greet(across)

    def mean(v):
        return jnp.sum(v, axis=1, keepdims=True) * (1.0 / v.shape[1])

    def normalise():
        v = in_ref[...].astype(F32)
        v = v - mean(v)
        root = lax.rsqrt(mean(v * v) + 1e-06)
        return v * root, root

    with jax.named_scope("weights"):
        for fetch in fetches:
            fetch.wait()
        eye = pick(18, 18, lambda r: r)
        blocks = [qkv_ref[w].astype(F32) for w in range(3)] + [dot_nt(eye, proj_ref[...])]
        w_all = jnp.concatenate([jnp.where(dp == 0, v[:, :144], v[:, 144:]) for v in blocks], axis=1)
        tail = jnp.concatenate([w_all[16:18, HD * g : HD * g + HD] for g in range(8)], axis=0)
        w_in[...] = jnp.concatenate([w_all[:16], tail], axis=1).astype(BF)

    with jax.named_scope("rows"):
        feature = lax.broadcasted_iota(jnp.int32, (1152, QF), 0)
        col = lax.broadcasted_iota(jnp.int32, (1, QF), 1)
        b, k = lax.div(col, GF), lax.rem(col, GF)
        from_col = jnp.where(k < 64, (k >> 4) * 288 + (k & 15), ((k - 64) >> 1) * 288 + 16 + (k & 1)) + b * 72
        from_col = jnp.where(k < 72, from_col, -100)
        for q in range(4):
            order[q] = jnp.where(feature == from_col + 18 * q, 1.0, 0.0).astype(BF)
        perm[0] = pick(256, 256, lambda r: ((r >> 1) & 1) * 128 + (r >> 4) * 8 + ((r >> 2) & 3) * 2 + (r & 1))
        perm[1] = pick(256, 256, lambda r: ((r >> 1) & 15) * 16 + (r >> 6) * 4 + ((r >> 5) & 1) * 2 + (r & 1))
        perm[2] = pick(256, 256, lambda r: ((r >> 1) & 1) * 128 + ((r >> 2) & 3) * 32 + (r >> 4) * 2 + (r & 1))
        perm[3] = pick(256, 256, lambda r: ((r >> 1) & 3) * 64 + (r >> 7) * 32 + ((r >> 3) & 15) * 2 + (r & 1))
        normed, _ = normalise()
        hidden_in = (normed * (1.0 + mod_ref[1:2]) + mod_ref[0:1]).astype(BF)
        d_branch = (mod_ref[2:3] * cot_ref[...].astype(F32)).astype(BF)
        quarter = dot(jnp.concatenate([hidden_in, d_branch], axis=0), order[hd]).astype(BF)
        rows_in[...] = dot(perm[0], quarter).astype(BF).reshape(NZ, 16, QF)

    with jax.named_scope("greeted"):
        pl.semaphore_wait(barrier, 37)

    with jax.named_scope("weights_4"):
        for i, d in enumerate((8, 4, -4)):
            send(w_in, w4.at[z // 4], S_W4 + i, at_z(d))
        z_send(lambda k: rows_in.at[k], r2, S_Z1)
        r2[z] = rows_in[z]
        w4[z // 4] = w_in[...]
        for i, d in enumerate((8, 4, -4)):
            landed(w4.at[mod(z // 4 - d // 4, 4)], S_W4 + i)
        tail = w4[:, :, WCOLS : WCOLS + HD].reshape(64, HD)
        tail = jnp.concatenate([tail] * 8, axis=1)
        pair = (lax.broadcasted_iota(jnp.int32, (64, WCOLS), 0) >> 1) & 7
        group = lax.div(lax.broadcasted_iota(jnp.int32, (1, WCOLS), 1), HD)
        tail = jnp.where(pair == group, tail.astype(F32), 0.0).astype(BF)
        r = lax.broadcasted_iota(jnp.int32, (16, 64), 0)
        c = lax.broadcasted_iota(jnp.int32, (16, 64), 1)
        gather = jnp.where(r == (c >> 4) * 2 + (c & 1), 1.0, 0.0).astype(BF)
        zq = mod(z, 4)
        xw[x, zq, 0:64] = w4[:, :, 0:WCOLS].reshape(64, WCOLS)
        xw[x, zq, 64:80] = dot(gather, tail).astype(BF)

    routes = [(dz, dx) for dx in (2, 1, 3, 0) for dz in ((2 if dx % 2 == 0 else -2), 1, -1, 0) if (dz, dx) != (0, 0)]
    with jax.named_scope("weights_near"):
        for i, (dz, dx) in enumerate(routes):
            send(xw.at[x, zq], xw.at[x, zq], S_WX + i, at_zx(dz, dx))

    with jax.named_scope("rows_z"):
        z_landed(r2, S_Z1)
        z1[...] = dot(perm[1], r2[...].reshape(256, QF)).astype(BF).reshape(NX, 64, QF)
        for d in (2, 1, 3):
            send(z1.at[mod(x + d, NX)], r1.at[x], S_X1 + d - 1, at_x(d))
        r1[x] = z1[x]

    with jax.named_scope("rows_x"):
        for d in range(1, NX):
            landed(r1.at[mod(x - d, NX)], S_X1 + d - 1)
        for arr in range(2):
            for k in range(NX):
                a[core, y, 128 * arr + 32 * k : 128 * arr + 32 * k + 32] = r1[k, 32 * arr : 32 * arr + 32]
        for d in (2, 1, 3):
            send(a.at[core, y], a.at[core, y], S_AY + d - 1, at_y(d))
        send(a.at[core, y], a.at[core, y], S_AC, across)

    with jax.named_scope("rows_y"):
        for d in (1, 3, 2):
            slot = a.at[core, mod(y - d, NY)]
            landed(slot, S_AY + d - 1)
            send(slot, slot, S_AC + d, across)
        for d in range(NY):
            landed(a.at[1 - core, mod(y - d, NY)], S_AC + d)

    def rows_of(q, arr):
        lo = arr * 128
        return jnp.concatenate([a[q % 2, (q // 2) * 2 + p, lo : lo + 128, :] for p in range(2)], axis=0)

    with jax.named_scope("project"):

        def weights(q):
            return xw[q].reshape(QF, WCOLS)

        def project(q):
            w = weights(q)
            return dot(rows_of(q, 0), w[:, :QKV]), dot(rows_of(q, 1), w[:, QKV:])

        raw, d_att = jnp.zeros((256, QKV), F32), jnp.zeros((256, 144), F32)
        for dx in (0, 1, 3, 2):
            q = mod(x - dx, NX)
            for i, (dz, dx_of) in enumerate(routes):
                if dx_of == dx:
                    landed(xw.at[q, mod(z - dz, 4)], S_WX + i)
            more_raw, more_d = project(q)
            raw, d_att = raw + more_raw, d_att + more_d
        d_att = d_att.astype(BF)

    q_gain, k_gain = qg_ref[...], kg_ref[...]
    factor = 1.0 / np.sqrt(np.float32(HD))
    row_i = lax.broadcasted_iota(jnp.int32, (128, 128), 0) % 2
    col_i = lax.broadcasted_iota(jnp.int32, (128, 128), 1) % 2
    same = row_i == col_i

    def norm(v, gain):
        root = lax.rsqrt(jnp.sum(v * v, axis=-1, keepdims=True) * (1.0 / HD) + 1e-06)
        return (v * root * gain).astype(BF), root

    def part_cols(v, p, k):
        return v[128 * p : 128 * p + 128, HD * k : HD * k + HD]

    with jax.named_scope("attend"):
        state, att = [], [[], []]
        for p in range(2):
            for h in range(2):
                rq, rk, v = (part_cols(raw, p, 2 * w + h) for w in range(3))
                v = v.astype(BF)
                qn, root_q = norm(rq, q_gain)
                kn, root_k = norm(rk, k_gain)
                s = jnp.where(same, dot_nt(qn, kn) * factor, -1e30)
                e = jnp.exp(s - jnp.max(s, axis=-1, keepdims=True))
                pr = e / jnp.sum(e, axis=-1, keepdims=True)
                pb = pr.astype(BF)
                att[p].append(dot(pb, v).astype(BF))
                state.append((rq, rk, v, qn, kn, root_q, root_k, pr, pb))
        att = [jnp.concatenate(half, axis=1) for half in att]

    def spread(q, val, buf):
        for p in range(2):
            buf[q % 2, (q // 2) * 2 + p] = val[128 * p : 128 * p + 128].astype(BF)

    with jax.named_scope("branch"):
        both = jnp.concatenate(att, axis=0)
        for q in range(4):
            spread(q, dot_nt(both, weights(q)[:, QKV:]), bp)
        send(bp.at[1 - core], bq, S_B, across)

    def to_y(own, got, total, far, base):
        landed(got, base)
        total[...] = (own[core].astype(F32) + got[...].astype(F32)).astype(BF)
        for d in (2, 1, 3):
            send(total.at[mod(y + d, NY)], far.at[d - 1], base + d, at_y(d))

    def y_sum(total, far, base):
        for d in range(1, NY):
            landed(far.at[d - 1], base + d)
        s = total[y].astype(F32)
        for d in range(1, NY):
            s += far[d - 1].astype(F32)
        return s

    with jax.named_scope("attend_back"):
        d_raw = []
        for p in range(2):
            cols_q, cols_k, cols_v = [], [], []
            for h in range(2):
                rq, rk, v, qn, kn, root_q, root_k, pr, pb = state[2 * p + h]
                da = part_cols(d_att, p, h)
                dv = dot_tn(pb, da).astype(BF)
                d_p = dot_nt(da, v)
                ds = (pr * (d_p - jnp.sum(pr * d_p, axis=-1, keepdims=True)) * factor).astype(BF)
                dq = dot(ds, kn).astype(BF)
                dk = dot_tn(ds, qn).astype(BF)

                def norm_back(v_raw, root, gain, d_n):
                    gq = gain * d_n.astype(F32)
                    inner = jnp.sum(v_raw * gq, axis=-1, keepdims=True) * (1.0 / HD)
                    return (root * gq - v_raw * (root * root * root) * inner).astype(BF)

                cols_q.append(norm_back(rq, root_q, q_gain, dq))
                cols_k.append(norm_back(rk, root_k, k_gain, dk))
                cols_v.append(dv)
            d_raw.append(jnp.concatenate(cols_q + cols_k + cols_v, axis=1))
        d_raw = jnp.concatenate(d_raw, axis=0)
        to_y(bp, bq, bt, bu, S_B)
        for q in range(4):
            spread(q, dot_nt(d_raw, weights(q)[:, :QKV]), hp)
        send(hp.at[1 - core], hq, S_H, across)

    with jax.named_scope("hidden_y"):
        to_y(hp, hq, ht, hu, S_H)

    with jax.named_scope("proj_grad"):
        none = jnp.zeros((128, 144), BF)
        att_c = jnp.concatenate(
            [jnp.concatenate([att[0], none], axis=1), jnp.concatenate([none, att[1]], axis=1)], axis=0
        )
        for q in range(4):
            px[q] = dot_tn(rows_of(q, 1), att_c).astype(BF)
        for d in (2, 1, 3):
            send(px.at[mod(x + d, NX)], pxr.at[d - 1], S_PX + d - 1, at_x(d))

    with jax.named_scope("back_z"):
        branch = y_sum(bt, bu, S_B)
        hidden = y_sum(ht, hu, S_H)
        both = jnp.concatenate([branch.astype(BF), hidden.astype(BF)], axis=0)
        zb[...] = dot(perm[2], both).astype(BF).reshape(NZ, 16, QF)
        z_send(lambda k: zb.at[k], r3, S_Z2)
        r3[z] = zb[z]

    with jax.named_scope("grad_x"):
        for d in range(1, NX):
            landed(pxr.at[d - 1], S_PX + d - 1)
        s = px[x].astype(F32)
        for d in range(1, NX):
            s += pxr[d - 1].astype(F32)
        body = jnp.concatenate([s[GF * b : GF * b + 64] for b in range(4)], axis=0)
        tail = jnp.concatenate([s[GF * b + 64 : GF * b + 72] for b in range(4)], axis=0).astype(BF)
        widen = pick(256, 32, lambda r: jnp.where((r & 15) < 8, (r >> 4) * 2 + ((r >> 2) & 1), -1))
        row4 = lax.broadcasted_iota(jnp.int32, (256, 288), 0) & 3
        group = lax.div(lax.broadcasted_iota(jnp.int32, (1, 288), 1), HD)
        tail = jnp.where(row4 == group, dot(widen, tail), 0.0)
        tail = tail[:, 0:72] + tail[:, 72:144] + tail[:, 144:216] + tail[:, 216:288]
        pz[...] = jnp.concatenate([body, tail], axis=1).astype(BF).reshape(NZ, 16, 360)
        z_send(lambda k: pz.at[lax.rem(k, 4) * 4 + k // 4], pzr, S_PZ)
        pzr[z] = pz[zq * 4 + z // 4]

    with jax.named_scope("back_x"):
        z_landed(r3, S_Z2)
        xs[...] = dot(perm[1], r3[...].reshape(256, QF)).astype(BF).reshape(NX, 64, QF)
        for d in (2, 1, 3):
            to = mod(x + d, NX)
            send(xs.at[to], r4.at[hd, x], S_XF + d, at_x_far(d))
            send(xs.at[to], r4.at[hd, x], S_X2 + d - 1, at_x(d))
        send(xs.at[x], r4.at[hd, x], S_XF, at_y(2))
        r4[hd, x] = xs[x]
        for d in range(1, NX):
            landed(r4.at[hd, mod(x - d, NX)], S_X2 + d - 1)
        send(r4.at[hd], r4.at[hd], S_OC, across)
        for d in range(NX):
            landed(r4.at[far_hd, mod(x - d, NX)], S_XF + d)
        send(r4.at[far_hd], r4.at[far_hd], S_OC + 1, across)

    with jax.named_scope("grad_z"):
        z_landed(pzr, S_PZ)
        s = pzr[0].astype(F32)
        for k in range(1, NZ):
            s += pzr[k].astype(F32)
        pgs[dp] = s
        send(pgs.at[dp], pgs.at[dp], S_PY, at_y(1 - 2 * dp))

    with jax.named_scope("results"):

        def natural(q):
            return dot_nt(dot(perm[3], r4[q].reshape(256, QF)).astype(BF), order[q])

        total = natural(hd) + natural(far_hd)
        landed(r4.at[hd + 1 - 2 * core], S_OC)
        total += natural(hd + 1 - 2 * core)
        landed(r4.at[mod(hd + 3 - 2 * core, 4)], S_OC + 1)
        total += natural(mod(hd + 3 - 2 * core, 4))
        out_ref[...] = (in_ref[...].astype(F32) + mod_ref[2:3] * total[0:128]).astype(BF)
        normed, root = normalise()
        d_n = total[128:256] * (1.0 + mod_ref[1:2])
        d_in = root * (d_n - mean(d_n) - normed * mean(d_n * normed))
        ig_ref[...] = (cot_ref[...].astype(F32) + d_in).astype(BF)
        landed(pgs.at[1 - dp], S_PY)
        pg_ref[...] = pgs[...]

    with jax.named_scope("sent"):
        for wait in sent:
            wait()


def per_device(inputs, modulation, qkv_weight, proj_weight, q_gain, k_gain, cotangent):
    dp = lax.axis_index("dp")
    tokens, width = inputs.shape[1:]

    def vm(*shape, dtype=BF):
        return pltpu.VMEM(shape, dtype)

    operands = (inputs[0], cotangent[0], modulation, qkv_weight, proj_weight, q_gain[None], k_gain[None])
    out, ig, pg = pl.pallas_call(
        kernel,
        out_shape=(
            jax.ShapeDtypeStruct((tokens, width), BF),
            jax.ShapeDtypeStruct((tokens, width), BF),
            jax.ShapeDtypeStruct((2, 16, 360), F32),
        ),
        in_specs=[pl.BlockSpec(memory_space=pl.ANY)] * 7,
        out_specs=[pl.BlockSpec(memory_space=pltpu.VMEM)] * 3,
        scratch_shapes=[
            *[vm(*v.shape, dtype=v.dtype) for v in operands],
            vm(4, 1152, QF),
            vm(4, 256, 256),
            vm(16, WCOLS + HD),
            vm(NZ, 16, QF),
            vm(NX, 64, QF),
            vm(4, 16, WCOLS + HD),
            vm(NX, 64, QF),
            vm(NZ, 16, QF),
            vm(NX, 4, GF, WCOLS),
            vm(2, NY, 256, QF),
            vm(2, NY, 128, QF),
            vm(NY, 128, QF),
            vm(NY, 128, QF),
            vm(3, 128, QF),
            vm(2, NY, 128, QF),
            vm(NY, 128, QF),
            vm(NY, 128, QF),
            vm(3, 128, QF),
            vm(NZ, 16, QF),
            vm(NZ, 16, QF),
            vm(NX, 64, QF),
            vm(4, NX, 64, QF),
            vm(NX, QF, 288),
            vm(3, QF, 288),
            vm(NZ, 16, 360),
            vm(NZ, 16, 360),
            vm(2, 16, 360, dtype=F32),
            pltpu.SemaphoreType.DMA((N_SEM,)),
            pltpu.SemaphoreType.DMA((N_SEM,)),
            pltpu.SemaphoreType.DMA((len(operands),)),
        ],
        compiler_params=pltpu.CompilerParams(
            collective_id=0, has_side_effects=True, vmem_limit_bytes=60 * 1024 * 1024
        ),
    )(*operands)

    pg = jnp.concatenate([pg[:, :, :288], pg[:, :8, 288:].reshape(2, 2, 288)], axis=1)
    pg = lax.dynamic_slice(pg, (0, 0, dp * 144), (2, 18, 144))
    proj_grad = pg.transpose(0, 2, 1).reshape(288, 18)
    return out[None], ig[None], proj_grad


def solution(mesh):
    return jax.shard_map(
        per_device,
        mesh=mesh,
        in_specs=(
            P(("dp", "frame"), None, None),
            P("dp", None),
            P(None, "frame", "head"),
            P("head", "frame"),
            P(),
            P(),
            P(("dp", "frame"), None, None),
        ),
        out_specs=(
            P(("dp", "frame"), None, None),
            P(("dp", "frame"), None, None),
            P(("dp", "head"), "frame"),
        ),
        check_vma=False,
    )
```

```python
import jax
import jax.numpy as jnp
import numpy as np
from jax import lax
from jax.experimental import pallas as pl
from jax.experimental.pallas import tpu as pltpu
from jax.sharding import PartitionSpec as P

MESH = pl.DeviceIdType.MESH
BF = jnp.bfloat16
F32 = jnp.float32
NZ, NX, NY = 16, 4, 4
HD = 72
GF = 80
QF = 4 * GF
QKV, WCOLS = 432, 576

S_Z1 = 0
S_X1 = S_Z1 + 15
S_W4 = S_X1 + 3
S_WX = S_W4 + 3
S_AY = S_WX + 16
S_AC = S_AY + 3
S_B = S_AC + 4
S_H = S_B + 4
S_Z2 = S_H + 4
S_X2 = S_Z2 + 15
S_XF = S_X2 + 3
S_OC = S_XF + 4
S_PX = S_OC + 2
S_PZ = S_PX + 3
S_PY = S_PZ + 15
N_SEM = S_PY + 1


def pick(rows, cols, source):
    r = lax.broadcasted_iota(jnp.int32, (rows, 1), 0)
    c = lax.broadcasted_iota(jnp.int32, (rows, cols), 1)
    return jnp.where(c == source(r), 1.0, 0.0).astype(BF)


def dot(a, b):
    return jnp.dot(a, b, preferred_element_type=F32)


def dot_nt(a, b):
    return lax.dot_general(a, b, (((1,), (1,)), ((), ())), preferred_element_type=F32)


def dot_tn(a, b):
    return lax.dot_general(a, b, (((0,), (0,)), ((), ())), preferred_element_type=F32)


def mod(a, n):
    return lax.rem(a + n, n)


def kernel(
    in_hbm, cot_hbm, mod_hbm, qkv_hbm, proj_hbm, qg_hbm, kg_hbm,
    out_ref, ig_ref, pg_ref,
    in_ref, cot_ref, mod_ref, qkv_ref, proj_ref, qg_ref, kg_ref,
    order, perm, w_in, rows_in, r1, w4, z1, r2, xw, a, bp, bq, bt, bu, hp, hq, ht, hu, zb, r3, xs, r4, px, pxr, pz, pzr, pgs,
    ss, rs, ls,
):
    fetches = [
        pltpu.make_async_copy(src, dst, ls.at[i])
        for i, (src, dst) in enumerate(
            [
                (qkv_hbm, qkv_ref), (proj_hbm, proj_ref), (in_hbm, in_ref), (cot_hbm, cot_ref),
                (mod_hbm, mod_ref), (qg_hbm, qg_ref), (kg_hbm, kg_ref),
            ]
        )
    ]
    for fetch in fetches:
        fetch.start()

    f, hd, dp = lax.axis_index("frame"), lax.axis_index("head"), lax.axis_index("dp")
    z, x = f // NX, lax.rem(f, NX)
    core, y = lax.rem(hd, 2), (hd // 2) * 2 + dp
    far_hd = mod(hd + 2, 4)

    def at_x(d):
        return (z * NX + mod(x + d, NX), hd, dp)

    def at_x_far(d):
        return (z * NX + mod(x + d, NX), far_hd, dp)

    def at_zx(dz, dx):
        return (mod(z + dz, NZ) * NX + mod(x + dx, NX), hd, dp)

    def at_z(d):
        return (mod(z + d, NZ) * NX + x, hd, dp)

    def at_y(d):
        yy = mod(y + d, NY)
        return (f, (yy // 2) * 2 + core, lax.rem(yy, 2))

    across = (f, hd + 1 - 2 * core, dp)

    def copy(src, dst, i, dev):
        return pltpu.make_async_remote_copy(
            src_ref=src, dst_ref=dst, send_sem=ss.at[i], recv_sem=rs.at[i], device_id=dev, device_id_type=MESH
        )

    sent = []

    def send(*args):
        c = copy(*args)
        c.start()
        sent.append(c.wait_send)

    def landed(ref, i):
        copy(ref, ref, i, across).wait_recv()

    def z_send(src_of, dst, base):
        def each(d, c):
            copy(src_of(mod(z + d, NZ)), dst.at[z], base + d - 1, at_z(d)).start()
            return c

        lax.fori_loop(1, NZ, each, 0)

        def each_sent(d, c):
            copy(src_of(mod(z + d, NZ)), dst.at[z], base + d - 1, at_z(d)).wait_send()
            return c

        sent.append(lambda: lax.fori_loop(1, NZ, each_sent, 0))

    def z_landed(dst, base):
        def each(d, c):
            landed(dst.at[mod(z - d, NZ)], base + d - 1)
            return c

        lax.fori_loop(1, NZ, each, 0)

    routes = [(dz, dx) for dx in (1, 3, 0) for dz in (0, 1, -1, -2 if dx == 3 else 2) if (dz, dx) != (0, 0)]
    barrier = pltpu.get_barrier_semaphore()

    def greet(dev):
        pl.semaphore_signal(barrier, inc=1, device_id=dev, device_id_type=MESH)

    with jax.named_scope("greet"):

        def greet_z(d, c):
            greet(at_z(d))
            return c

        lax.fori_loop(1, NZ, greet_z, 0)
        for d in range(1, NX):
            greet(at_x(d))
            greet(at_x_far(d))
        for dz, dx in routes:
            if dx and dz:
                greet(at_zx(dz, dx))
        for d in range(1, NY):
            greet(at_y(d))
        greet(across)

    def mean(v):
        return jnp.sum(v, axis=1, keepdims=True) * (1.0 / v.shape[1])

    def normalise():
        v = in_ref[...].astype(F32)
        v = v - mean(v)
        root = lax.rsqrt(mean(v * v) + 1e-06)
        return v * root, root

    with jax.named_scope("weights"):
        for fetch in fetches:
            fetch.wait()
        blocks = [qkv_ref[w].astype(F32) for w in range(3)] + [proj_ref[...].astype(F32)]
        w_all = jnp.concatenate([jnp.where(dp == 0, v[:, :144], v[:, 144:]) for v in blocks], axis=1)
        tail = jnp.concatenate([w_all[16:18, HD * g : HD * g + HD] for g in range(8)], axis=0)
        w_in[...] = jnp.concatenate([w_all[:16], tail], axis=1).astype(BF)

    with jax.named_scope("rows"):
        feature = lax.broadcasted_iota(jnp.int32, (1152, QF), 0)
        col = lax.broadcasted_iota(jnp.int32, (1, QF), 1)
        b, k = lax.div(col, GF), lax.rem(col, GF)
        from_col = jnp.where(k < 64, (k >> 4) * 288 + (k & 15), ((k - 64) >> 1) * 288 + 16 + (k & 1)) + b * 72
        from_col = jnp.where(k < 72, from_col, -100)
        for q in range(4):
            order[q] = jnp.where(feature == from_col + 18 * q, 1.0, 0.0).astype(BF)
        perm[0] = pick(256, 256, lambda r: ((r >> 1) & 1) * 128 + (r >> 4) * 8 + ((r >> 2) & 3) * 2 + (r & 1))
        perm[1] = pick(256, 256, lambda r: ((r >> 1) & 15) * 16 + (r >> 6) * 4 + ((r >> 5) & 1) * 2 + (r & 1))
        perm[2] = pick(256, 256, lambda r: ((r >> 1) & 1) * 128 + ((r >> 2) & 3) * 32 + (r >> 4) * 2 + (r & 1))
        perm[3] = pick(256, 256, lambda r: ((r >> 1) & 3) * 64 + (r >> 7) * 32 + ((r >> 3) & 15) * 2 + (r & 1))
        normed, _ = normalise()
        hidden_in = (normed * (1.0 + mod_ref[1:2]) + mod_ref[0:1]).astype(BF)
        d_branch = (mod_ref[2:3] * cot_ref[...].astype(F32)).astype(BF)
        quarter = dot(jnp.concatenate([hidden_in, d_branch], axis=0), order[hd]).astype(BF)
        rows_in[...] = dot(perm[0], quarter).astype(BF).reshape(NZ, 16, QF)

    with jax.named_scope("greeted"):
        pl.semaphore_wait(barrier, 31)

    zq = mod(z, 4)

    def send_near(lo, hi):
        for i in range(lo, hi):
            send(xw.at[x, zq], xw.at[x, zq], S_WX + i, at_zx(*routes[i]))

    def near_landed(dx):
        for i, (dz, dx_of) in enumerate(routes):
            if dx_of == dx:
                landed(xw.at[mod(x - dx, NX), mod(z - dz, 4)], S_WX + i)

    with jax.named_scope("rows_z"):
        z_send(lambda k: rows_in.at[k], r2, S_Z1)
        for i, d in enumerate((8, 4, -4)):
            send(w_in, w4.at[z // 4], S_W4 + i, at_z(d))
        r2[z] = rows_in[z]
        w4[z // 4] = w_in[...]
        z_landed(r2, S_Z1)
        z1[...] = dot(perm[1], r2[...].reshape(256, QF)).astype(BF).reshape(NX, 64, QF)
        for d in (2, 1, 3):
            send(z1.at[mod(x + d, NX)], r1.at[x], S_X1 + d - 1, at_x(d))
        r1[x] = z1[x]

    with jax.named_scope("weights_4"):
        for i, d in enumerate((8, 4, -4)):
            landed(w4.at[mod(z // 4 - d // 4, 4)], S_W4 + i)
        tail = w4[:, :, WCOLS : WCOLS + HD].reshape(64, HD)
        tail = jnp.concatenate([tail] * 8, axis=1)
        pair = (lax.broadcasted_iota(jnp.int32, (64, WCOLS), 0) >> 1) & 7
        group = lax.div(lax.broadcasted_iota(jnp.int32, (1, WCOLS), 1), HD)
        tail = jnp.where(pair == group, tail.astype(F32), 0.0).astype(BF)
        r = lax.broadcasted_iota(jnp.int32, (16, 64), 0)
        c = lax.broadcasted_iota(jnp.int32, (16, 64), 1)
        gather = jnp.where(r == (c >> 4) * 2 + (c & 1), 1.0, 0.0).astype(BF)
        xw[x, zq, 0:64] = w4[:, :, 0:WCOLS].reshape(64, WCOLS)
        xw[x, zq, 64:80] = dot(gather, tail).astype(BF)
        send_near(0, 8)

    with jax.named_scope("rows_x"):
        for d in range(1, NX):
            landed(r1.at[mod(x - d, NX)], S_X1 + d - 1)
        for arr in range(2):
            for k in range(NX):
                a[core, y, 128 * arr + 32 * k : 128 * arr + 32 * k + 32] = r1[k, 32 * arr : 32 * arr + 32]
        for d in (2, 1, 3):
            send(a.at[core, y], a.at[core, y], S_AY + d - 1, at_y(d))
        send(a.at[core, y], a.at[core, y], S_AC, across)

    with jax.named_scope("weights_near"):
        send_near(8, len(routes))
        near_landed(1)
        for i, dz in enumerate((0, 1)):
            slot = xw.at[mod(x - 1, NX), mod(z - dz, 4)]
            send(slot, slot, S_WX + 11 + i, at_x(1))
        near_landed(3)
        for i, dz in enumerate((-1, -2)):
            slot = xw.at[mod(x + 1, NX), mod(z - dz, 4)]
            send(slot, slot, S_WX + 13 + i, at_x(-1))

    with jax.named_scope("rows_y"):
        for d in (1, 3, 2):
            slot = a.at[core, mod(y - d, NY)]
            landed(slot, S_AY + d - 1)
            send(slot, slot, S_AC + d, across)
        for d in range(NY):
            landed(a.at[1 - core, mod(y - d, NY)], S_AC + d)

    def rows_of(q, arr):
        lo = arr * 128
        return jnp.concatenate([a[q % 2, (q // 2) * 2 + p, lo : lo + 128, :] for p in range(2)], axis=0)

    with jax.named_scope("project"):

        def weights(q):
            return xw[q].reshape(QF, WCOLS)

        def project(q):
            w = weights(q)
            return dot(rows_of(q, 0), w[:, :QKV]), dot(rows_of(q, 1), w[:, QKV:])

        raw, d_att = jnp.zeros((256, QKV), F32), jnp.zeros((256, 144), F32)
        for dx in (1, 3, 0, 2):
            q = mod(x - dx, NX)
            if dx == 0:
                near_landed(0)
            if dx == 2:
                for i, dz in enumerate((0, 1, -1, -2)):
                    landed(xw.at[q, mod(z - dz, 4)], S_WX + 11 + i)
            more_raw, more_d = project(q)
            raw, d_att = raw + more_raw, d_att + more_d
        d_att = d_att.astype(BF)

    q_gain, k_gain = qg_ref[...], kg_ref[...]
    factor = 1.0 / np.sqrt(np.float32(HD))
    row_i = lax.broadcasted_iota(jnp.int32, (128, 128), 0) % 2
    col_i = lax.broadcasted_iota(jnp.int32, (128, 128), 1) % 2
    same = row_i == col_i

    def norm(v, gain):
        root = lax.rsqrt(jnp.sum(v * v, axis=-1, keepdims=True) * (1.0 / HD) + 1e-06)
        return (v * root * gain).astype(BF), root

    def part_cols(v, p, k):
        return v[128 * p : 128 * p + 128, HD * k : HD * k + HD]

    with jax.named_scope("attend"):
        state, att = [], [[], []]
        for p in range(2):
            for h in range(2):
                rq, rk, v = (part_cols(raw, p, 2 * w + h) for w in range(3))
                v = v.astype(BF)
                qn, root_q = norm(rq, q_gain)
                kn, root_k = norm(rk, k_gain)
                s = jnp.where(same, dot_nt(qn, kn) * factor, -1e30)
                e = jnp.exp(s - jnp.max(s, axis=-1, keepdims=True))
                pr = e / jnp.sum(e, axis=-1, keepdims=True)
                pb = pr.astype(BF)
                att[p].append(dot(pb, v).astype(BF))
                state.append((rq, rk, v, qn, kn, root_q, root_k, pr, pb))
        att = [jnp.concatenate(half, axis=1) for half in att]

    def spread(q, val, buf):
        for p in range(2):
            buf[q % 2, (q // 2) * 2 + p] = val[128 * p : 128 * p + 128].astype(BF)

    with jax.named_scope("branch"):
        both = jnp.concatenate(att, axis=0)
        for q in range(4):
            spread(q, dot_nt(both, weights(q)[:, QKV:]), bp)
        send(bp.at[1 - core], bq, S_B, across)

    def to_y(own, got, total, far, base):
        landed(got, base)
        total[...] = (own[core].astype(F32) + got[...].astype(F32)).astype(BF)
        for d in (2, 1, 3):
            send(total.at[mod(y + d, NY)], far.at[d - 1], base + d, at_y(d))

    def y_sum(total, far, base):
        for d in range(1, NY):
            landed(far.at[d - 1], base + d)
        s = total[y].astype(F32)
        for d in range(1, NY):
            s += far[d - 1].astype(F32)
        return s

    with jax.named_scope("attend_back"):
        d_raw = []
        for p in range(2):
            cols_q, cols_k, cols_v = [], [], []
            for h in range(2):
                rq, rk, v, qn, kn, root_q, root_k, pr, pb = state[2 * p + h]
                da = part_cols(d_att, p, h)
                dv = dot_tn(pb, da).astype(BF)
                d_p = dot_nt(da, v)
                ds = (pr * (d_p - jnp.sum(pr * d_p, axis=-1, keepdims=True)) * factor).astype(BF)
                dq = dot(ds, kn).astype(BF)
                dk = dot_tn(ds, qn).astype(BF)

                def norm_back(v_raw, root, gain, d_n):
                    gq = gain * d_n.astype(F32)
                    inner = jnp.sum(v_raw * gq, axis=-1, keepdims=True) * (1.0 / HD)
                    return (root * gq - v_raw * (root * root * root) * inner).astype(BF)

                cols_q.append(norm_back(rq, root_q, q_gain, dq))
                cols_k.append(norm_back(rk, root_k, k_gain, dk))
                cols_v.append(dv)
            d_raw.append(jnp.concatenate(cols_q + cols_k + cols_v, axis=1))
        d_raw = jnp.concatenate(d_raw, axis=0)
        to_y(bp, bq, bt, bu, S_B)
        for q in range(4):
            spread(q, dot_nt(d_raw, weights(q)[:, :QKV]), hp)
        send(hp.at[1 - core], hq, S_H, across)

    with jax.named_scope("proj_grad"):
        none = jnp.zeros((128, 144), BF)
        att_c = jnp.concatenate(
            [jnp.concatenate([att[0], none], axis=1), jnp.concatenate([none, att[1]], axis=1)], axis=0
        )
        for q in range(4):
            px[q] = dot_tn(rows_of(q, 1), att_c).astype(BF)
        for d in (2, 1, 3):
            send(px.at[mod(x + d, NX)], pxr.at[d - 1], S_PX + d - 1, at_x(d))

    with jax.named_scope("hidden_y"):
        to_y(hp, hq, ht, hu, S_H)

    with jax.named_scope("back_z"):
        branch = y_sum(bt, bu, S_B)
        hidden = y_sum(ht, hu, S_H)
        both = jnp.concatenate([branch.astype(BF), hidden.astype(BF)], axis=0)
        zb[...] = dot(perm[2], both).astype(BF).reshape(NZ, 16, QF)
        z_send(lambda k: zb.at[k], r3, S_Z2)
        r3[z] = zb[z]

    with jax.named_scope("grad_x"):
        for d in range(1, NX):
            landed(pxr.at[d - 1], S_PX + d - 1)
        s = px[x].astype(F32)
        for d in range(1, NX):
            s += pxr[d - 1].astype(F32)
        body = jnp.concatenate([s[GF * b : GF * b + 64] for b in range(4)], axis=0)
        tail = jnp.concatenate([s[GF * b + 64 : GF * b + 72] for b in range(4)], axis=0).astype(BF)
        widen = pick(256, 32, lambda r: jnp.where((r & 15) < 8, (r >> 4) * 2 + ((r >> 2) & 1), -1))
        row4 = lax.broadcasted_iota(jnp.int32, (256, 288), 0) & 3
        group = lax.div(lax.broadcasted_iota(jnp.int32, (1, 288), 1), HD)
        tail = jnp.where(row4 == group, dot(widen, tail), 0.0)
        tail = tail[:, 0:72] + tail[:, 72:144] + tail[:, 144:216] + tail[:, 216:288]
        pz[...] = jnp.concatenate([body, tail], axis=1).astype(BF).reshape(NZ, 16, 360)
        z_send(lambda k: pz.at[lax.rem(k, 4) * 4 + k // 4], pzr, S_PZ)
        pzr[z] = pz[zq * 4 + z // 4]

    with jax.named_scope("back_x"):
        z_landed(r3, S_Z2)
        xs[...] = dot(perm[1], r3[...].reshape(256, QF)).astype(BF).reshape(NX, 64, QF)
        for d in (2, 1, 3):
            to = mod(x + d, NX)
            send(xs.at[to], r4.at[hd, x], S_XF + d, at_x_far(d))
            send(xs.at[to], r4.at[hd, x], S_X2 + d - 1, at_x(d))
        send(xs.at[x], r4.at[hd, x], S_XF, at_y(2))
        r4[hd, x] = xs[x]
        for d in range(1, NX):
            landed(r4.at[hd, mod(x - d, NX)], S_X2 + d - 1)
        send(r4.at[hd], r4.at[hd], S_OC, across)
        for d in range(NX):
            landed(r4.at[far_hd, mod(x - d, NX)], S_XF + d)
        send(r4.at[far_hd], r4.at[far_hd], S_OC + 1, across)

    with jax.named_scope("grad_z"):
        z_landed(pzr, S_PZ)
        s = pzr[0].astype(F32)
        for k in range(1, NZ):
            s += pzr[k].astype(F32)
        pgs[dp] = s
        send(pgs.at[dp], pgs.at[dp], S_PY, at_y(1 - 2 * dp))

    with jax.named_scope("results"):

        def natural(q):
            return dot_nt(dot(perm[3], r4[q].reshape(256, QF)).astype(BF), order[q])

        total = natural(hd) + natural(far_hd)
        landed(r4.at[hd + 1 - 2 * core], S_OC)
        total += natural(hd + 1 - 2 * core)
        landed(r4.at[mod(hd + 3 - 2 * core, 4)], S_OC + 1)
        total += natural(mod(hd + 3 - 2 * core, 4))
        out_ref[...] = (in_ref[...].astype(F32) + mod_ref[2:3] * total[0:128]).astype(BF)
        normed, root = normalise()
        d_n = total[128:256] * (1.0 + mod_ref[1:2])
        d_in = root * (d_n - mean(d_n) - normed * mean(d_n * normed))
        ig_ref[...] = (cot_ref[...].astype(F32) + d_in).astype(BF)
        landed(pgs.at[1 - dp], S_PY)
        halves = []
        for v in (pgs[0], pgs[1]):
            last = [
                jnp.concatenate([jnp.concatenate([v[r + k : r + k + 1, 288:360] for k in range(2)], axis=1) for r in (o, o + 4)], axis=0)
                for o in (0, 2)
            ]
            parts = [jnp.concatenate([v[:, 144 * p : 144 * p + 144], last[p]], axis=0) for p in range(2)]
            halves.append(jnp.where(dp == 0, parts[0], parts[1]))
        pg_ref[...] = jnp.concatenate(halves, axis=1)

    with jax.named_scope("sent"):
        for wait in sent:
            wait()


def per_device(inputs, modulation, qkv_weight, proj_weight, q_gain, k_gain, cotangent):
    tokens, width = inputs.shape[1:]

    def vm(*shape, dtype=BF):
        return pltpu.VMEM(shape, dtype)

    operands = (inputs[0], cotangent[0], modulation, qkv_weight, proj_weight.T, q_gain[None], k_gain[None])
    out, ig, pg = pl.pallas_call(
        kernel,
        out_shape=(
            jax.ShapeDtypeStruct((tokens, width), BF),
            jax.ShapeDtypeStruct((tokens, width), BF),
            jax.ShapeDtypeStruct((18, 288), F32),
        ),
        in_specs=[pl.BlockSpec(memory_space=pl.ANY)] * 7,
        out_specs=[pl.BlockSpec(memory_space=pltpu.VMEM)] * 3,
        scratch_shapes=[
            *[vm(*v.shape, dtype=v.dtype) for v in operands],
            vm(4, 1152, QF),
            vm(4, 256, 256),
            vm(16, WCOLS + HD),
            vm(NZ, 16, QF),
            vm(NX, 64, QF),
            vm(4, 16, WCOLS + HD),
            vm(NX, 64, QF),
            vm(NZ, 16, QF),
            vm(NX, 4, GF, WCOLS),
            vm(2, NY, 256, QF),
            vm(2, NY, 128, QF),
            vm(NY, 128, QF),
            vm(NY, 128, QF),
            vm(3, 128, QF),
            vm(2, NY, 128, QF),
            vm(NY, 128, QF),
            vm(NY, 128, QF),
            vm(3, 128, QF),
            vm(NZ, 16, QF),
            vm(NZ, 16, QF),
            vm(NX, 64, QF),
            vm(4, NX, 64, QF),
            vm(NX, QF, 288),
            vm(3, QF, 288),
            vm(NZ, 16, 360),
            vm(NZ, 16, 360),
            vm(2, 16, 360, dtype=F32),
            pltpu.SemaphoreType.DMA((N_SEM,)),
            pltpu.SemaphoreType.DMA((N_SEM,)),
            pltpu.SemaphoreType.DMA((len(operands),)),
        ],
        compiler_params=pltpu.CompilerParams(
            collective_id=0, has_side_effects=True, vmem_limit_bytes=60 * 1024 * 1024
        ),
    )(*operands)

    return out[None], ig[None], pg.T


def solution(mesh):
    return jax.shard_map(
        per_device,
        mesh=mesh,
        in_specs=(
            P(("dp", "frame"), None, None),
            P("dp", None),
            P(None, "frame", "head"),
            P("head", "frame"),
            P(),
            P(),
            P(("dp", "frame"), None, None),
        ),
        out_specs=(
            P(("dp", "frame"), None, None),
            P(("dp", "frame"), None, None),
            P(("dp", "head"), "frame"),
        ),
        check_vma=False,
    )
```

```python
import jax
import jax.numpy as jnp
import numpy as np
from jax import lax
from jax.experimental import pallas as pl
from jax.experimental.pallas import tpu as pltpu
from jax.sharding import PartitionSpec as P

MESH = pl.DeviceIdType.MESH
BF = jnp.bfloat16
F32 = jnp.float32
NZ, NX, NY = 16, 4, 4
HD = 72
GF = 80
QF = 4 * GF
QKV, WCOLS = 432, 576

S_Z1 = 0
S_X1 = S_Z1 + 15
S_W4 = S_X1 + 3
S_WX = S_W4 + 3
S_AY = S_WX + 16
S_AC = S_AY + 3
S_B = S_AC + 4
S_H = S_B + 4
S_Z2 = S_H + 4
S_X2 = S_Z2 + 15
S_XF = S_X2 + 3
S_OC = S_XF + 4
S_PX = S_OC + 2
S_PZ = S_PX + 3
S_PY = S_PZ + 15
N_SEM = S_PY + 1


def pick(rows, cols, source):
    r = lax.broadcasted_iota(jnp.int32, (rows, 1), 0)
    c = lax.broadcasted_iota(jnp.int32, (rows, cols), 1)
    return jnp.where(c == source(r), 1.0, 0.0).astype(BF)


def dot(a, b):
    return jnp.dot(a, b, preferred_element_type=F32)


def dot_nt(a, b):
    return lax.dot_general(a, b, (((1,), (1,)), ((), ())), preferred_element_type=F32)


def dot_tn(a, b):
    return lax.dot_general(a, b, (((0,), (0,)), ((), ())), preferred_element_type=F32)


def mod(a, n):
    return lax.rem(a + n, n)


def kernel(
    in_hbm, cot_hbm, mod_hbm, qkv_hbm, proj_hbm, qg_hbm, kg_hbm,
    out_ref, ig_ref, pg_ref,
    in_ref, cot_ref, mod_ref, qkv_ref, proj_ref, qg_ref, kg_ref,
    order, perm, w_in, rows_in, r1, w4, z1, r2, xw, a, bp, bq, bt, bu, hp, hq, ht, hu, zb, r3, xs, r4, px, pxr, pz, pzr, pgs,
    ss, rs, ls,
):
    fetches = [
        pltpu.make_async_copy(src, dst, ls.at[i])
        for i, (src, dst) in enumerate(
            [
                (qkv_hbm, qkv_ref), (proj_hbm, proj_ref), (in_hbm, in_ref), (cot_hbm, cot_ref),
                (mod_hbm, mod_ref), (qg_hbm, qg_ref), (kg_hbm, kg_ref),
            ]
        )
    ]
    for fetch in fetches:
        fetch.start()

    f, hd, dp = lax.axis_index("frame"), lax.axis_index("head"), lax.axis_index("dp")
    z, x = f // NX, lax.rem(f, NX)
    core, y = lax.rem(hd, 2), (hd // 2) * 2 + dp
    far_hd = mod(hd + 2, 4)

    def at_x(d):
        return (z * NX + mod(x + d, NX), hd, dp)

    def at_x_far(d):
        return (z * NX + mod(x + d, NX), far_hd, dp)

    def at_zx(dz, dx):
        return (mod(z + dz, NZ) * NX + mod(x + dx, NX), hd, dp)

    def at_z(d):
        return (mod(z + d, NZ) * NX + x, hd, dp)

    def at_y(d):
        yy = mod(y + d, NY)
        return (f, (yy // 2) * 2 + core, lax.rem(yy, 2))

    across = (f, hd + 1 - 2 * core, dp)

    def copy(src, dst, i, dev):
        return pltpu.make_async_remote_copy(
            src_ref=src, dst_ref=dst, send_sem=ss.at[i], recv_sem=rs.at[i], device_id=dev, device_id_type=MESH
        )

    sent = []

    def send(*args):
        c = copy(*args)
        c.start()
        sent.append(c.wait_send)

    def landed(ref, i):
        copy(ref, ref, i, across).wait_recv()

    def z_send(src_of, dst, base):
        def each(d, c):
            copy(src_of(mod(z + d, NZ)), dst.at[z], base + d - 1, at_z(d)).start()
            return c

        lax.fori_loop(1, NZ, each, 0)

        def each_sent(d, c):
            copy(src_of(mod(z + d, NZ)), dst.at[z], base + d - 1, at_z(d)).wait_send()
            return c

        sent.append(lambda: lax.fori_loop(1, NZ, each_sent, 0))

    def z_landed(dst, base):
        def each(d, c):
            landed(dst.at[mod(z - d, NZ)], base + d - 1)
            return c

        lax.fori_loop(1, NZ, each, 0)

    routes = [(-2, 3), (1, 1), (-1, 3), (0, 1), (2, 1), (0, 3), (-1, 1), (1, 3), (2, 0), (1, 0), (-1, 0)]
    barrier = pltpu.get_barrier_semaphore()

    def greet(dev):
        pl.semaphore_signal(barrier, inc=1, device_id=dev, device_id_type=MESH)

    with jax.named_scope("greet"):

        def greet_z(d, c):
            greet(at_z(d))
            return c

        lax.fori_loop(1, NZ, greet_z, 0)
        for d in range(1, NX):
            greet(at_x(d))
            greet(at_x_far(d))
        for dz, dx in routes:
            if dx and dz:
                greet(at_zx(dz, dx))
        for d in range(1, NY):
            greet(at_y(d))
        greet(across)

    def mean(v):
        return jnp.sum(v, axis=1, keepdims=True) * (1.0 / v.shape[1])

    def normalise():
        v = in_ref[...].astype(F32)
        v = v - mean(v)
        root = lax.rsqrt(mean(v * v) + 1e-06)
        return v * root, root

    with jax.named_scope("weights"):
        for fetch in fetches:
            fetch.wait()
        blocks = [qkv_ref[w].astype(F32) for w in range(3)] + [proj_ref[...].astype(F32)]
        w_all = jnp.concatenate([jnp.where(dp == 0, v[:, :144], v[:, 144:]) for v in blocks], axis=1)
        tail = jnp.concatenate([w_all[16:18, HD * g : HD * g + HD] for g in range(8)], axis=0)
        w_in[...] = jnp.concatenate([w_all[:16], tail], axis=1).astype(BF)

    with jax.named_scope("rows"):
        feature = lax.broadcasted_iota(jnp.int32, (1152, QF), 0)
        col = lax.broadcasted_iota(jnp.int32, (1, QF), 1)
        b, k = lax.div(col, GF), lax.rem(col, GF)
        from_col = jnp.where(k < 64, (k >> 4) * 288 + (k & 15), ((k - 64) >> 1) * 288 + 16 + (k & 1)) + b * 72
        from_col = jnp.where(k < 72, from_col, -100)
        for q in range(4):
            order[q] = jnp.where(feature == from_col + 18 * q, 1.0, 0.0).astype(BF)
        perm[0] = pick(256, 256, lambda r: ((r >> 1) & 1) * 128 + (r >> 4) * 8 + ((r >> 2) & 3) * 2 + (r & 1))
        perm[1] = pick(256, 256, lambda r: ((r >> 1) & 15) * 16 + (r >> 6) * 4 + ((r >> 5) & 1) * 2 + (r & 1))
        perm[2] = pick(256, 256, lambda r: ((r >> 1) & 1) * 128 + ((r >> 2) & 3) * 32 + (r >> 4) * 2 + (r & 1))
        perm[3] = pick(256, 256, lambda r: ((r >> 1) & 3) * 64 + (r >> 7) * 32 + ((r >> 3) & 15) * 2 + (r & 1))
        normed, _ = normalise()
        hidden_in = (normed * (1.0 + mod_ref[1:2]) + mod_ref[0:1]).astype(BF)
        d_branch = (mod_ref[2:3] * cot_ref[...].astype(F32)).astype(BF)
        quarter = dot(jnp.concatenate([hidden_in, d_branch], axis=0), order[hd]).astype(BF)
        rows_in[...] = dot(perm[0], quarter).astype(BF).reshape(NZ, 16, QF)

    with jax.named_scope("greeted"):
        pl.semaphore_wait(barrier, 31)

    zq = mod(z, 4)

    def send_near(lo, hi):
        for i in range(lo, hi):
            send(xw.at[x, zq], xw.at[x, zq], S_WX + i, at_zx(*routes[i]))

    def near_landed(i):
        dz, dx = routes[i]
        slot = xw.at[mod(x - dx, NX), mod(z - dz, 4)]
        landed(slot, S_WX + i)
        return slot

    with jax.named_scope("rows_z"):
        z_send(lambda k: rows_in.at[k], r2, S_Z1)
        for i, d in enumerate((8, 4, -4)):
            send(w_in, w4.at[z // 4], S_W4 + i, at_z(d))
        r2[z] = rows_in[z]
        w4[z // 4] = w_in[...]
        z_landed(r2, S_Z1)
        z1[...] = dot(perm[1], r2[...].reshape(256, QF)).astype(BF).reshape(NX, 64, QF)
        for d in (2, 1, 3):
            send(z1.at[mod(x + d, NX)], r1.at[x], S_X1 + d - 1, at_x(d))
        r1[x] = z1[x]

    with jax.named_scope("weights_4"):
        for i, d in enumerate((8, 4, -4)):
            landed(w4.at[mod(z // 4 - d // 4, 4)], S_W4 + i)
        tail = w4[:, :, WCOLS : WCOLS + HD].reshape(64, HD)
        tail = jnp.concatenate([tail] * 8, axis=1)
        pair = (lax.broadcasted_iota(jnp.int32, (64, WCOLS), 0) >> 1) & 7
        group = lax.div(lax.broadcasted_iota(jnp.int32, (1, WCOLS), 1), HD)
        tail = jnp.where(pair == group, tail.astype(F32), 0.0).astype(BF)
        r = lax.broadcasted_iota(jnp.int32, (16, 64), 0)
        c = lax.broadcasted_iota(jnp.int32, (16, 64), 1)
        gather = jnp.where(r == (c >> 4) * 2 + (c & 1), 1.0, 0.0).astype(BF)
        xw[x, zq, 0:64] = w4[:, :, 0:WCOLS].reshape(64, WCOLS)
        xw[x, zq, 64:80] = dot(gather, tail).astype(BF)
        send_near(0, 8)

    with jax.named_scope("rows_x"):
        for d in range(1, NX):
            landed(r1.at[mod(x - d, NX)], S_X1 + d - 1)
        for arr in range(2):
            for k in range(NX):
                a[core, y, 128 * arr + 32 * k : 128 * arr + 32 * k + 32] = r1[k, 32 * arr : 32 * arr + 32]
        for d in (2, 1, 3):
            send(a.at[core, y], a.at[core, y], S_AY + d - 1, at_y(d))
        send(a.at[core, y], a.at[core, y], S_AC, across)

    with jax.named_scope("weights_near"):
        send_near(8, len(routes))
        for i in range(4):
            slot = near_landed(i)
            send(slot, slot, S_WX + 11 + i, at_x(routes[i][1] if routes[i][1] == 1 else -1))

    with jax.named_scope("rows_y"):
        for d in (1, 3, 2):
            slot = a.at[core, mod(y - d, NY)]
            landed(slot, S_AY + d - 1)
            send(slot, slot, S_AC + d, across)
        for d in range(NY):
            landed(a.at[1 - core, mod(y - d, NY)], S_AC + d)

    def rows_of(q, arr):
        lo = arr * 128
        return jnp.concatenate([a[q % 2, (q // 2) * 2 + p, lo : lo + 128, :] for p in range(2)], axis=0)

    with jax.named_scope("project"):

        def weights(q):
            return xw[q].reshape(QF, WCOLS)

        def project(q):
            w = weights(q)
            return dot(rows_of(q, 0), w[:, :QKV]), dot(rows_of(q, 1), w[:, QKV:])

        raw, d_att = jnp.zeros((256, QKV), F32), jnp.zeros((256, 144), F32)
        for dx in (1, 3, 0, 2):
            q = mod(x - dx, NX)
            for i in range(4, len(routes)):
                if routes[i][1] == dx:
                    near_landed(i)
            if dx == 2:
                for i in range(4):
                    landed(xw.at[q, mod(z - routes[i][0], 4)], S_WX + 11 + i)
            more_raw, more_d = project(q)
            raw, d_att = raw + more_raw, d_att + more_d
        d_att = d_att.astype(BF)

    q_gain, k_gain = qg_ref[...], kg_ref[...]
    factor = 1.0 / np.sqrt(np.float32(HD))
    row_i = lax.broadcasted_iota(jnp.int32, (128, 128), 0) % 2
    col_i = lax.broadcasted_iota(jnp.int32, (128, 128), 1) % 2
    same = row_i == col_i

    def norm(v, gain):
        root = lax.rsqrt(jnp.sum(v * v, axis=-1, keepdims=True) * (1.0 / HD) + 1e-06)
        return (v * root * gain).astype(BF), root

    def part_cols(v, p, k):
        return v[128 * p : 128 * p + 128, HD * k : HD * k + HD]

    with jax.named_scope("attend"):
        state, att = [], [[], []]
        for p in range(2):
            for h in range(2):
                rq, rk, v = (part_cols(raw, p, 2 * w + h) for w in range(3))
                v = v.astype(BF)
                qn, root_q = norm(rq, q_gain)
                kn, root_k = norm(rk, k_gain)
                s = jnp.where(same, dot_nt(qn, kn) * factor, -1e30)
                e = jnp.exp(s - jnp.max(s, axis=-1, keepdims=True))
                pr = e / jnp.sum(e, axis=-1, keepdims=True)
                pb = pr.astype(BF)
                att[p].append(dot(pb, v).astype(BF))
                state.append((rq, rk, v, qn, kn, root_q, root_k, pr, pb))
        att = [jnp.concatenate(half, axis=1) for half in att]

    def spread(q, val, buf):
        for p in range(2):
            buf[q % 2, (q // 2) * 2 + p] = val[128 * p : 128 * p + 128].astype(BF)

    with jax.named_scope("branch"):
        both = jnp.concatenate(att, axis=0)
        for q in range(4):
            spread(q, dot_nt(both, weights(q)[:, QKV:]), bp)
        send(bp.at[1 - core], bq, S_B, across)

    def to_y(own, got, total, far, base):
        landed(got, base)
        total[...] = (own[core].astype(F32) + got[...].astype(F32)).astype(BF)
        for d in (2, 1, 3):
            send(total.at[mod(y + d, NY)], far.at[d - 1], base + d, at_y(d))

    def y_sum(total, far, base):
        for d in range(1, NY):
            landed(far.at[d - 1], base + d)
        s = total[y].astype(F32)
        for d in range(1, NY):
            s += far[d - 1].astype(F32)
        return s

    with jax.named_scope("branch_y"):
        to_y(bp, bq, bt, bu, S_B)

    with jax.named_scope("attend_back"):
        d_raw = []
        for p in range(2):
            cols_q, cols_k, cols_v = [], [], []
            for h in range(2):
                rq, rk, v, qn, kn, root_q, root_k, pr, pb = state[2 * p + h]
                da = part_cols(d_att, p, h)
                dv = dot_tn(pb, da).astype(BF)
                d_p = dot_nt(da, v)
                ds = (pr * (d_p - jnp.sum(pr * d_p, axis=-1, keepdims=True)) * factor).astype(BF)
                dq = dot(ds, kn).astype(BF)
                dk = dot_tn(ds, qn).astype(BF)

                def norm_back(v_raw, root, gain, d_n):
                    gq = gain * d_n.astype(F32)
                    inner = jnp.sum(v_raw * gq, axis=-1, keepdims=True) * (1.0 / HD)
                    return (root * gq - v_raw * (root * root * root) * inner).astype(BF)

                cols_q.append(norm_back(rq, root_q, q_gain, dq))
                cols_k.append(norm_back(rk, root_k, k_gain, dk))
                cols_v.append(dv)
            d_raw.append(jnp.concatenate(cols_q + cols_k + cols_v, axis=1))
        d_raw = jnp.concatenate(d_raw, axis=0)
        for q in range(4):
            spread(q, dot_nt(d_raw, weights(q)[:, :QKV]), hp)
        send(hp.at[1 - core], hq, S_H, across)

    with jax.named_scope("proj_grad"):
        none = jnp.zeros((128, 144), BF)
        att_c = jnp.concatenate(
            [jnp.concatenate([att[0], none], axis=1), jnp.concatenate([none, att[1]], axis=1)], axis=0
        )
        for q in range(4):
            px[q] = dot_tn(rows_of(q, 1), att_c).astype(BF)
        for d in (2, 1, 3):
            send(px.at[mod(x + d, NX)], pxr.at[d - 1], S_PX + d - 1, at_x(d))

    with jax.named_scope("hidden_y"):
        to_y(hp, hq, ht, hu, S_H)

    with jax.named_scope("back_z"):
        branch = y_sum(bt, bu, S_B)
        hidden = y_sum(ht, hu, S_H)
        both = jnp.concatenate([branch.astype(BF), hidden.astype(BF)], axis=0)
        zb[...] = dot(perm[2], both).astype(BF).reshape(NZ, 16, QF)
        z_send(lambda k: zb.at[k], r3, S_Z2)
        r3[z] = zb[z]

    with jax.named_scope("grad_x"):
        for d in range(1, NX):
            landed(pxr.at[d - 1], S_PX + d - 1)
        s = px[x].astype(F32)
        for d in range(1, NX):
            s += pxr[d - 1].astype(F32)
        body = jnp.concatenate([s[GF * b : GF * b + 64] for b in range(4)], axis=0)
        tail = jnp.concatenate([s[GF * b + 64 : GF * b + 72] for b in range(4)], axis=0).astype(BF)
        widen = pick(256, 32, lambda r: jnp.where((r & 15) < 8, (r >> 4) * 2 + ((r >> 2) & 1), -1))
        row4 = lax.broadcasted_iota(jnp.int32, (256, 288), 0) & 3
        group = lax.div(lax.broadcasted_iota(jnp.int32, (1, 288), 1), HD)
        tail = jnp.where(row4 == group, dot(widen, tail), 0.0)
        tail = tail[:, 0:72] + tail[:, 72:144] + tail[:, 144:216] + tail[:, 216:288]
        pz[...] = jnp.concatenate([body, tail], axis=1).astype(BF).reshape(NZ, 16, 360)
        z_send(lambda k: pz.at[lax.rem(k, 4) * 4 + k // 4], pzr, S_PZ)
        pzr[z] = pz[zq * 4 + z // 4]

    with jax.named_scope("back_x"):
        z_landed(r3, S_Z2)
        xs[...] = dot(perm[1], r3[...].reshape(256, QF)).astype(BF).reshape(NX, 64, QF)
        for d in (2, 1, 3):
            to = mod(x + d, NX)
            send(xs.at[to], r4.at[hd, x], S_XF + d, at_x_far(d))
            send(xs.at[to], r4.at[hd, x], S_X2 + d - 1, at_x(d))
        send(xs.at[x], r4.at[hd, x], S_XF, at_y(2))
        r4[hd, x] = xs[x]
        for d in range(1, NX):
            landed(r4.at[hd, mod(x - d, NX)], S_X2 + d - 1)
        send(r4.at[hd], r4.at[hd], S_OC, across)
        for d in range(NX):
            landed(r4.at[far_hd, mod(x - d, NX)], S_XF + d)
        send(r4.at[far_hd], r4.at[far_hd], S_OC + 1, across)

    with jax.named_scope("grad_z"):
        z_landed(pzr, S_PZ)
        s = pzr[0].astype(F32)
        for k in range(1, NZ):
            s += pzr[k].astype(F32)
        pgs[dp] = s
        send(pgs.at[dp], pgs.at[dp], S_PY, at_y(1 - 2 * dp))

    with jax.named_scope("results"):

        def natural(q):
            return dot_nt(dot(perm[3], r4[q].reshape(256, QF)).astype(BF), order[q])

        normed, root = normalise()
        total = natural(hd) + natural(far_hd)
        landed(r4.at[hd + 1 - 2 * core], S_OC)
        total += natural(hd + 1 - 2 * core)
        landed(r4.at[mod(hd + 3 - 2 * core, 4)], S_OC + 1)
        total += natural(mod(hd + 3 - 2 * core, 4))
        out_ref[...] = (in_ref[...].astype(F32) + mod_ref[2:3] * total[0:128]).astype(BF)
        d_n = total[128:256] * (1.0 + mod_ref[1:2])
        d_in = root * (d_n - mean(d_n) - normed * mean(d_n * normed))
        ig_ref[...] = (cot_ref[...].astype(F32) + d_in).astype(BF)
        landed(pgs.at[1 - dp], S_PY)
        halves = []
        for v in (pgs[0], pgs[1]):
            last = [
                jnp.concatenate([jnp.concatenate([v[r + k : r + k + 1, 288:360] for k in range(2)], axis=1) for r in (o, o + 4)], axis=0)
                for o in (0, 2)
            ]
            parts = [jnp.concatenate([v[:, 144 * p : 144 * p + 144], last[p]], axis=0) for p in range(2)]
            halves.append(jnp.where(dp == 0, parts[0], parts[1]))
        pg_ref[...] = jnp.concatenate(halves, axis=1)

    with jax.named_scope("sent"):
        for wait in sent:
            wait()


def per_device(inputs, modulation, qkv_weight, proj_weight, q_gain, k_gain, cotangent):
    tokens, width = inputs.shape[1:]

    def vm(*shape, dtype=BF):
        return pltpu.VMEM(shape, dtype)

    operands = (inputs[0], cotangent[0], modulation, qkv_weight, proj_weight.T, q_gain[None], k_gain[None])
    out, ig, pg = pl.pallas_call(
        kernel,
        out_shape=(
            jax.ShapeDtypeStruct((tokens, width), BF),
            jax.ShapeDtypeStruct((tokens, width), BF),
            jax.ShapeDtypeStruct((18, 288), F32),
        ),
        in_specs=[pl.BlockSpec(memory_space=pl.ANY)] * 7,
        out_specs=[pl.BlockSpec(memory_space=pltpu.VMEM)] * 3,
        scratch_shapes=[
            *[vm(*v.shape, dtype=v.dtype) for v in operands],
            vm(4, 1152, QF),
            vm(4, 256, 256),
            vm(16, WCOLS + HD),
            vm(NZ, 16, QF),
            vm(NX, 64, QF),
            vm(4, 16, WCOLS + HD),
            vm(NX, 64, QF),
            vm(NZ, 16, QF),
            vm(NX, 4, GF, WCOLS),
            vm(2, NY, 256, QF),
            vm(2, NY, 128, QF),
            vm(NY, 128, QF),
            vm(NY, 128, QF),
            vm(3, 128, QF),
            vm(2, NY, 128, QF),
            vm(NY, 128, QF),
            vm(NY, 128, QF),
            vm(3, 128, QF),
            vm(NZ, 16, QF),
            vm(NZ, 16, QF),
            vm(NX, 64, QF),
            vm(4, NX, 64, QF),
            vm(NX, QF, 288),
            vm(3, QF, 288),
            vm(NZ, 16, 360),
            vm(NZ, 16, 360),
            vm(2, 16, 360, dtype=F32),
            pltpu.SemaphoreType.DMA((N_SEM,)),
            pltpu.SemaphoreType.DMA((N_SEM,)),
            pltpu.SemaphoreType.DMA((len(operands),)),
        ],
        compiler_params=pltpu.CompilerParams(
            collective_id=0, has_side_effects=True, vmem_limit_bytes=60 * 1024 * 1024
        ),
    )(*operands)

    return out[None], ig[None], pg.T


def solution(mesh):
    return jax.shard_map(
        per_device,
        mesh=mesh,
        in_specs=(
            P(("dp", "frame"), None, None),
            P("dp", None),
            P(None, "frame", "head"),
            P("head", "frame"),
            P(),
            P(),
            P(("dp", "frame"), None, None),
        ),
        out_specs=(
            P(("dp", "frame"), None, None),
            P(("dp", "frame"), None, None),
            P(("dp", "head"), "frame"),
        ),
        check_vma=False,
    )
```

```python
import jax
import jax.numpy as jnp
import numpy as np
from jax import lax
from jax.experimental import pallas as pl
from jax.experimental.pallas import tpu as pltpu
from jax.sharding import PartitionSpec as P

MESH = pl.DeviceIdType.MESH
BF = jnp.bfloat16
F32 = jnp.float32
NZ, NX, NY = 16, 4, 4
HD = 72
GF = 80
QF = 4 * GF
QKV, WCOLS = 432, 576

S_Z1 = 0
S_X1 = S_Z1 + 15
S_W4 = S_X1 + 3
S_WX = S_W4 + 3
S_AY = S_WX + 16
S_AC = S_AY + 3
S_B = S_AC + 4
S_H = S_B + 4
S_Z2 = S_H + 4
S_X2 = S_Z2 + 15
S_XF = S_X2 + 3
S_OC = S_XF + 4
S_PX = S_OC + 2
S_PZ = S_PX + 3
S_PY = S_PZ + 15
N_SEM = S_PY + 1


def pick(rows, cols, source):
    r = lax.broadcasted_iota(jnp.int32, (rows, 1), 0)
    c = lax.broadcasted_iota(jnp.int32, (rows, cols), 1)
    return jnp.where(c == source(r), 1.0, 0.0).astype(BF)


def dot(a, b):
    return jnp.dot(a, b, preferred_element_type=F32)


def dot_nt(a, b):
    return lax.dot_general(a, b, (((1,), (1,)), ((), ())), preferred_element_type=F32)


def dot_tn(a, b):
    return lax.dot_general(a, b, (((0,), (0,)), ((), ())), preferred_element_type=F32)


def mod(a, n):
    return lax.rem(a + n, n)


def kernel(
    in_hbm, cot_hbm, mod_hbm, qkv_hbm, proj_hbm, qg_hbm, kg_hbm,
    out_ref, ig_ref, pg_ref,
    in_ref, cot_ref, mod_ref, qkv_ref, proj_ref, qg_ref, kg_ref,
    order, perm, w_in, rows_in, r1, w4, z1, r2, xw, a, bp, bq, bt, bu, hp, hq, ht, hu, zb, r3, xs, r4, px, pxr, pz, pzr, pgs,
    ss, rs, ls,
):
    fetches = [
        pltpu.make_async_copy(src, dst, ls.at[i])
        for i, (src, dst) in enumerate(
            [
                (qkv_hbm, qkv_ref), (proj_hbm, proj_ref), (in_hbm, in_ref), (cot_hbm, cot_ref),
                (mod_hbm, mod_ref), (qg_hbm, qg_ref), (kg_hbm, kg_ref),
            ]
        )
    ]
    for fetch in fetches:
        fetch.start()

    f, hd, dp = lax.axis_index("frame"), lax.axis_index("head"), lax.axis_index("dp")
    z, x = f // NX, lax.rem(f, NX)
    core, y = lax.rem(hd, 2), (hd // 2) * 2 + dp
    far_hd = mod(hd + 2, 4)

    def at_x(d):
        return (z * NX + mod(x + d, NX), hd, dp)

    def at_x_far(d):
        return (z * NX + mod(x + d, NX), far_hd, dp)

    def at_zx(dz, dx):
        return (mod(z + dz, NZ) * NX + mod(x + dx, NX), hd, dp)

    def at_z(d):
        return (mod(z + d, NZ) * NX + x, hd, dp)

    def at_y(d):
        yy = mod(y + d, NY)
        return (f, (yy // 2) * 2 + core, lax.rem(yy, 2))

    across = (f, hd + 1 - 2 * core, dp)

    def copy(src, dst, i, dev):
        return pltpu.make_async_remote_copy(
            src_ref=src, dst_ref=dst, send_sem=ss.at[i], recv_sem=rs.at[i], device_id=dev, device_id_type=MESH
        )

    sent = []

    def send(*args):
        c = copy(*args)
        c.start()
        sent.append(c.wait_send)

    def landed(ref, i):
        copy(ref, ref, i, across).wait_recv()

    def z_send(src_of, dst, base):
        def each(d, c):
            copy(src_of(mod(z + d, NZ)), dst.at[z], base + d - 1, at_z(d)).start()
            return c

        lax.fori_loop(1, NZ, each, 0)

        def each_sent(d, c):
            copy(src_of(mod(z + d, NZ)), dst.at[z], base + d - 1, at_z(d)).wait_send()
            return c

        sent.append(lambda: lax.fori_loop(1, NZ, each_sent, 0))

    def z_landed(dst, base):
        def each(d, c):
            landed(dst.at[mod(z - d, NZ)], base + d - 1)
            return c

        lax.fori_loop(1, NZ, each, 0)

    routes = [(-2, 3), (1, 1), (-1, 3), (0, 1), (2, 1), (0, 3), (-1, 1), (1, 3), (2, 0), (1, 0), (-1, 0)]
    barrier = pltpu.get_barrier_semaphore()

    def greet(dev):
        pl.semaphore_signal(barrier, inc=1, device_id=dev, device_id_type=MESH)

    with jax.named_scope("greet"):

        def greet_z(d, c):
            greet(at_z(d))
            return c

        lax.fori_loop(1, NZ, greet_z, 0)
        for d in range(1, NX):
            greet(at_x(d))
            greet(at_x_far(d))
        for dz, dx in routes:
            if dx and dz:
                greet(at_zx(dz, dx))
        for d in range(1, NY):
            greet(at_y(d))
        greet(across)

    def mean(v):
        return jnp.sum(v, axis=1, keepdims=True) * (1.0 / v.shape[1])

    def normalise():
        v = in_ref[...].astype(F32)
        v = v - mean(v)
        root = lax.rsqrt(mean(v * v) + 1e-06)
        return v * root, root

    with jax.named_scope("weights"):
        for fetch in fetches:
            fetch.wait()
        blocks = [qkv_ref[w].astype(F32) for w in range(3)] + [proj_ref[...].astype(F32)]
        w_all = jnp.concatenate([jnp.where(dp == 0, v[:, :144], v[:, 144:]) for v in blocks], axis=1)
        tail = jnp.concatenate([w_all[16:18, HD * g : HD * g + HD] for g in range(8)], axis=0)
        w_in[...] = jnp.concatenate([w_all[:16], tail], axis=1).astype(BF)

    with jax.named_scope("rows"):
        feature = lax.broadcasted_iota(jnp.int32, (1152, QF), 0)
        col = lax.broadcasted_iota(jnp.int32, (1, QF), 1)
        b, k = lax.div(col, GF), lax.rem(col, GF)
        from_col = jnp.where(k < 64, (k >> 4) * 288 + (k & 15), ((k - 64) >> 1) * 288 + 16 + (k & 1)) + b * 72
        from_col = jnp.where(k < 72, from_col, -100)
        for q in range(4):
            order[q] = jnp.where(feature == from_col + 18 * q, 1.0, 0.0).astype(BF)
        perm[0] = pick(256, 256, lambda r: ((r >> 1) & 1) * 128 + (r >> 4) * 8 + ((r >> 2) & 3) * 2 + (r & 1))
        perm[1] = pick(256, 256, lambda r: ((r >> 1) & 15) * 16 + (r >> 6) * 4 + ((r >> 5) & 1) * 2 + (r & 1))
        perm[2] = pick(256, 256, lambda r: ((r >> 1) & 1) * 128 + ((r >> 2) & 3) * 32 + (r >> 4) * 2 + (r & 1))
        perm[3] = pick(256, 256, lambda r: ((r >> 1) & 3) * 64 + (r >> 7) * 32 + ((r >> 3) & 15) * 2 + (r & 1))
        normed, _ = normalise()
        hidden_in = (normed * (1.0 + mod_ref[1:2]) + mod_ref[0:1]).astype(BF)
        d_branch = (mod_ref[2:3] * cot_ref[...].astype(F32)).astype(BF)
        quarter = dot(jnp.concatenate([hidden_in, d_branch], axis=0), order[hd]).astype(BF)
        rows_in[...] = dot(perm[0], quarter).astype(BF).reshape(NZ, 16, QF)

    with jax.named_scope("greeted"):
        pl.semaphore_wait(barrier, 31)

    zq = mod(z, 4)

    def send_near(lo, hi):
        for i in range(lo, hi):
            send(xw.at[x, zq], xw.at[x, zq], S_WX + i, at_zx(*routes[i]))

    def near_landed(i):
        dz, dx = routes[i]
        slot = xw.at[mod(x - dx, NX), mod(z - dz, 4)]
        landed(slot, S_WX + i)
        return slot

    with jax.named_scope("rows_z"):
        z_send(lambda k: rows_in.at[k], r2, S_Z1)
        for i, d in enumerate((8, 4, -4)):
            send(w_in, w4.at[z // 4], S_W4 + i, at_z(d))
        r2[z] = rows_in[z]
        w4[z // 4] = w_in[...]
        z_landed(r2, S_Z1)
        z1[...] = dot(perm[1], r2[...].reshape(256, QF)).astype(BF).reshape(NX, 64, QF)
        for d in (2, 1, 3):
            send(z1.at[mod(x + d, NX)], r1.at[x], S_X1 + d - 1, at_x(d))
        r1[x] = z1[x]

    with jax.named_scope("weights_4"):
        for i, d in enumerate((8, 4, -4)):
            landed(w4.at[mod(z // 4 - d // 4, 4)], S_W4 + i)
        tail = w4[:, :, WCOLS : WCOLS + HD].reshape(64, HD)
        tail = jnp.concatenate([tail] * 8, axis=1)
        pair = (lax.broadcasted_iota(jnp.int32, (64, WCOLS), 0) >> 1) & 7
        group = lax.div(lax.broadcasted_iota(jnp.int32, (1, WCOLS), 1), HD)
        tail = jnp.where(pair == group, tail.astype(F32), 0.0).astype(BF)
        r = lax.broadcasted_iota(jnp.int32, (16, 64), 0)
        c = lax.broadcasted_iota(jnp.int32, (16, 64), 1)
        gather = jnp.where(r == (c >> 4) * 2 + (c & 1), 1.0, 0.0).astype(BF)
        xw[x, zq, 0:64] = w4[:, :, 0:WCOLS].reshape(64, WCOLS)
        xw[x, zq, 64:80] = dot(gather, tail).astype(BF)
        send_near(0, 8)

    with jax.named_scope("rows_x"):
        for d in range(1, NX):
            landed(r1.at[mod(x - d, NX)], S_X1 + d - 1)
        for arr in range(2):
            for k in range(NX):
                a[core, y, 128 * arr + 32 * k : 128 * arr + 32 * k + 32] = r1[k, 32 * arr : 32 * arr + 32]
        for d in (2, 1, 3):
            send(a.at[core, y], a.at[core, y], S_AY + d - 1, at_y(d))
        send(a.at[core, y], a.at[core, y], S_AC, across)

    with jax.named_scope("weights_near"):
        send_near(8, len(routes))
        for i in range(4):
            slot = near_landed(i)
            send(slot, slot, S_WX + 11 + i, at_x(routes[i][1] if routes[i][1] == 1 else -1))

    with jax.named_scope("rows_y"):
        for d in (1, 3, 2):
            slot = a.at[core, mod(y - d, NY)]
            landed(slot, S_AY + d - 1)
            send(slot, slot, S_AC + d, across)
        for d in range(NY):
            landed(a.at[1 - core, mod(y - d, NY)], S_AC + d)

    def rows_of(q, arr):
        lo = arr * 128
        return jnp.concatenate([a[q % 2, (q // 2) * 2 + p, lo : lo + 128, :] for p in range(2)], axis=0)

    with jax.named_scope("project"):

        def weights(q):
            return xw[q].reshape(QF, WCOLS)

        def project(q):
            w = weights(q)
            return dot(rows_of(q, 0), w[:, :QKV]), dot(rows_of(q, 1), w[:, QKV:])

        raw, d_att = jnp.zeros((256, QKV), F32), jnp.zeros((256, 144), F32)
        for dx in (1, 3, 0, 2):
            q = mod(x - dx, NX)
            for i in range(4, len(routes)):
                if routes[i][1] == dx:
                    near_landed(i)
            if dx == 2:
                for i in range(4):
                    landed(xw.at[q, mod(z - routes[i][0], 4)], S_WX + 11 + i)
            more_raw, more_d = project(q)
            raw, d_att = raw + more_raw, d_att + more_d
        d_att = d_att.astype(BF)

    q_gain, k_gain = qg_ref[...], kg_ref[...]
    factor = 1.0 / np.sqrt(np.float32(HD))
    row_i = lax.broadcasted_iota(jnp.int32, (128, 128), 0) % 2
    col_i = lax.broadcasted_iota(jnp.int32, (128, 128), 1) % 2
    same = row_i == col_i

    def norm(v, gain):
        root = lax.rsqrt(jnp.sum(v * v, axis=-1, keepdims=True) * (1.0 / HD) + 1e-06)
        return (v * root * gain).astype(BF), root

    def part_cols(v, p, k):
        return v[128 * p : 128 * p + 128, HD * k : HD * k + HD]

    with jax.named_scope("attend"):
        state, att = [], [[], []]
        for p in range(2):
            for h in range(2):
                rq, rk, v = (part_cols(raw, p, 2 * w + h) for w in range(3))
                v = v.astype(BF)
                qn, root_q = norm(rq, q_gain)
                kn, root_k = norm(rk, k_gain)
                s = jnp.where(same, dot_nt(qn, kn) * factor, -1e30)
                e = jnp.exp(s - jnp.max(s, axis=-1, keepdims=True))
                pr = e / jnp.sum(e, axis=-1, keepdims=True)
                pb = pr.astype(BF)
                att[p].append(dot(pb, v).astype(BF))
                state.append((rq, rk, v, qn, kn, root_q, root_k, pr, pb))
        att = [jnp.concatenate(half, axis=1) for half in att]

    def spread(q, val, buf):
        for p in range(2):
            buf[q % 2, (q // 2) * 2 + p] = val[128 * p : 128 * p + 128].astype(BF)

    with jax.named_scope("branch"):
        both = jnp.concatenate(att, axis=0)
        for q in range(4):
            spread(q, dot_nt(both, weights(q)[:, QKV:]), bp)
        send(bp.at[1 - core], bq, S_B, across)

    def to_y(own, got, total, far, base):
        landed(got, base)
        total[...] = (own[core].astype(F32) + got[...].astype(F32)).astype(BF)
        for d in (2, 1, 3):
            send(total.at[mod(y + d, NY)], far.at[d - 1], base + d, at_y(d))

    def y_sum(total, far, base):
        for d in range(1, NY):
            landed(far.at[d - 1], base + d)
        s = total[y].astype(F32)
        for d in range(1, NY):
            s += far[d - 1].astype(F32)
        return s

    with jax.named_scope("branch_y"):
        to_y(bp, bq, bt, bu, S_B)

    with jax.named_scope("attend_back"):
        d_raw = []
        for p in range(2):
            cols_q, cols_k, cols_v = [], [], []
            for h in range(2):
                rq, rk, v, qn, kn, root_q, root_k, pr, pb = state[2 * p + h]
                da = part_cols(d_att, p, h)
                dv = dot_tn(pb, da).astype(BF)
                d_p = dot_nt(da, v)
                ds = (pr * (d_p - jnp.sum(pr * d_p, axis=-1, keepdims=True)) * factor).astype(BF)
                dq = dot(ds, kn).astype(BF)
                dk = dot_tn(ds, qn).astype(BF)

                def norm_back(v_raw, root, gain, d_n):
                    gq = gain * d_n.astype(F32)
                    inner = jnp.sum(v_raw * gq, axis=-1, keepdims=True) * (1.0 / HD)
                    return (root * gq - v_raw * (root * root * root) * inner).astype(BF)

                cols_q.append(norm_back(rq, root_q, q_gain, dq))
                cols_k.append(norm_back(rk, root_k, k_gain, dk))
                cols_v.append(dv)
            d_raw.append(jnp.concatenate(cols_q + cols_k + cols_v, axis=1))
        d_raw = jnp.concatenate(d_raw, axis=0)
        for k in range(4):
            q = mod(1 - core, 2) + 2 * k if k < 2 else core + 2 * (k - 2)
            spread(q, dot_nt(d_raw, weights(q)[:, :QKV]), hp)
            if k == 1:
                send(hp.at[1 - core], hq, S_H, across)

    with jax.named_scope("proj_grad"):
        none = jnp.zeros((128, 144), BF)
        att_c = jnp.concatenate(
            [jnp.concatenate([att[0], none], axis=1), jnp.concatenate([none, att[1]], axis=1)], axis=0
        )
        for q in range(4):
            px[q] = dot_tn(rows_of(q, 1), att_c).astype(BF)
        for d in (2, 1, 3):
            send(px.at[mod(x + d, NX)], pxr.at[d - 1], S_PX + d - 1, at_x(d))

    with jax.named_scope("hidden_y"):
        to_y(hp, hq, ht, hu, S_H)

    with jax.named_scope("back_z"):
        branch = y_sum(bt, bu, S_B)
        hidden = y_sum(ht, hu, S_H)
        both = jnp.concatenate([branch.astype(BF), hidden.astype(BF)], axis=0)
        zb[...] = dot(perm[2], both).astype(BF).reshape(NZ, 16, QF)
        z_send(lambda k: zb.at[k], r3, S_Z2)
        r3[z] = zb[z]

    with jax.named_scope("grad_x"):
        for d in range(1, NX):
            landed(pxr.at[d - 1], S_PX + d - 1)
        s = px[x].astype(F32)
        for d in range(1, NX):
            s += pxr[d - 1].astype(F32)
        body = jnp.concatenate([s[GF * b : GF * b + 64] for b in range(4)], axis=0)
        tail = jnp.concatenate([s[GF * b + 64 : GF * b + 72] for b in range(4)], axis=0).astype(BF)
        widen = pick(256, 32, lambda r: jnp.where((r & 15) < 8, (r >> 4) * 2 + ((r >> 2) & 1), -1))
        row4 = lax.broadcasted_iota(jnp.int32, (256, 288), 0) & 3
        group = lax.div(lax.broadcasted_iota(jnp.int32, (1, 288), 1), HD)
        tail = jnp.where(row4 == group, dot(widen, tail), 0.0)
        tail = tail[:, 0:72] + tail[:, 72:144] + tail[:, 144:216] + tail[:, 216:288]
        pz[...] = jnp.concatenate([body, tail], axis=1).astype(BF).reshape(NZ, 16, 360)
        z_send(lambda k: pz.at[lax.rem(k, 4) * 4 + k // 4], pzr, S_PZ)
        pzr[z] = pz[zq * 4 + z // 4]

    with jax.named_scope("back_x"):
        z_landed(r3, S_Z2)
        xs[...] = dot(perm[1], r3[...].reshape(256, QF)).astype(BF).reshape(NX, 64, QF)
        for d in (2, 1, 3):
            to = mod(x + d, NX)
            send(xs.at[to], r4.at[hd, x], S_XF + d, at_x_far(d))
            send(xs.at[to], r4.at[hd, x], S_X2 + d - 1, at_x(d))
        send(xs.at[x], r4.at[hd, x], S_XF, at_y(2))
        r4[hd, x] = xs[x]
        for d in range(1, NX):
            landed(r4.at[hd, mod(x - d, NX)], S_X2 + d - 1)
        send(r4.at[hd], r4.at[hd], S_OC, across)
        for d in range(NX):
            landed(r4.at[far_hd, mod(x - d, NX)], S_XF + d)
        send(r4.at[far_hd], r4.at[far_hd], S_OC + 1, across)

    with jax.named_scope("grad_z"):
        z_landed(pzr, S_PZ)
        s = pzr[0].astype(F32)
        for k in range(1, NZ):
            s += pzr[k].astype(F32)
        pgs[dp] = s
        send(pgs.at[dp], pgs.at[dp], S_PY, at_y(1 - 2 * dp))

    with jax.named_scope("results"):

        def natural(q):
            return dot_nt(dot(perm[3], r4[q].reshape(256, QF)).astype(BF), order[q])

        normed, root = normalise()
        total = natural(hd) + natural(far_hd)
        landed(r4.at[hd + 1 - 2 * core], S_OC)
        total += natural(hd + 1 - 2 * core)
        landed(r4.at[mod(hd + 3 - 2 * core, 4)], S_OC + 1)
        total += natural(mod(hd + 3 - 2 * core, 4))
        out_ref[...] = (in_ref[...].astype(F32) + mod_ref[2:3] * total[0:128]).astype(BF)
        d_n = total[128:256] * (1.0 + mod_ref[1:2])
        d_in = root * (d_n - mean(d_n) - normed * mean(d_n * normed))
        ig_ref[...] = (cot_ref[...].astype(F32) + d_in).astype(BF)
        landed(pgs.at[1 - dp], S_PY)
        halves = []
        for v in (pgs[0], pgs[1]):
            last = [
                jnp.concatenate([jnp.concatenate([v[r + k : r + k + 1, 288:360] for k in range(2)], axis=1) for r in (o, o + 4)], axis=0)
                for o in (0, 2)
            ]
            parts = [jnp.concatenate([v[:, 144 * p : 144 * p + 144], last[p]], axis=0) for p in range(2)]
            halves.append(jnp.where(dp == 0, parts[0], parts[1]))
        pg_ref[0:18, 0:288] = jnp.concatenate(halves, axis=1)

    with jax.named_scope("sent"):
        for wait in sent:
            wait()


def per_device(inputs, modulation, qkv_weight, proj_weight, q_gain, k_gain, cotangent):
    tokens, width = inputs.shape[1:]

    def vm(*shape, dtype=BF):
        return pltpu.VMEM(shape, dtype)

    operands = (inputs[0], cotangent[0], modulation, qkv_weight, proj_weight.T, q_gain[None], k_gain[None])
    out, ig, pg = pl.pallas_call(
        kernel,
        out_shape=(
            jax.ShapeDtypeStruct((tokens, width), BF),
            jax.ShapeDtypeStruct((tokens, width), BF),
            jax.ShapeDtypeStruct((24, 384), F32),
        ),
        in_specs=[pl.BlockSpec(memory_space=pl.ANY)] * 7,
        out_specs=[pl.BlockSpec(memory_space=pltpu.VMEM)] * 3,
        scratch_shapes=[
            *[vm(*v.shape, dtype=v.dtype) for v in operands],
            vm(4, 1152, QF),
            vm(4, 256, 256),
            vm(16, WCOLS + HD),
            vm(NZ, 16, QF),
            vm(NX, 64, QF),
            vm(4, 16, WCOLS + HD),
            vm(NX, 64, QF),
            vm(NZ, 16, QF),
            vm(NX, 4, GF, WCOLS),
            vm(2, NY, 256, QF),
            vm(2, NY, 128, QF),
            vm(NY, 128, QF),
            vm(NY, 128, QF),
            vm(3, 128, QF),
            vm(2, NY, 128, QF),
            vm(NY, 128, QF),
            vm(NY, 128, QF),
            vm(3, 128, QF),
            vm(NZ, 16, QF),
            vm(NZ, 16, QF),
            vm(NX, 64, QF),
            vm(4, NX, 64, QF),
            vm(NX, QF, 288),
            vm(3, QF, 288),
            vm(NZ, 16, 360),
            vm(NZ, 16, 360),
            vm(2, 16, 360, dtype=F32),
            pltpu.SemaphoreType.DMA((N_SEM,)),
            pltpu.SemaphoreType.DMA((N_SEM,)),
            pltpu.SemaphoreType.DMA((len(operands),)),
        ],
        compiler_params=pltpu.CompilerParams(
            collective_id=0, has_side_effects=True, vmem_limit_bytes=60 * 1024 * 1024
        ),
    )(*operands)

    return out[None], ig[None], pg[:18, :288].T


def solution(mesh):
    return jax.shard_map(
        per_device,
        mesh=mesh,
        in_specs=(
            P(("dp", "frame"), None, None),
            P("dp", None),
            P(None, "frame", "head"),
            P("head", "frame"),
            P(),
            P(),
            P(("dp", "frame"), None, None),
        ),
        out_specs=(
            P(("dp", "frame"), None, None),
            P(("dp", "frame"), None, None),
            P(("dp", "head"), "frame"),
        ),
        check_vma=False,
    )
```

```python
import jax
import jax.numpy as jnp
import numpy as np
from jax import lax
from jax.experimental import pallas as pl
from jax.experimental.pallas import tpu as pltpu
from jax.sharding import PartitionSpec as P

MESH = pl.DeviceIdType.MESH
BF = jnp.bfloat16
F32 = jnp.float32
NZ, NX, NY = 16, 4, 4
HD = 72
GF = 80
QF = 4 * GF
QKV, WCOLS = 432, 576

S_Z1 = 0
S_X1 = S_Z1 + 15
S_W4 = S_X1 + 3
S_WX = S_W4 + 3
S_AY = S_WX + 16
S_AC = S_AY + 3
S_B = S_AC + 4
S_H = S_B + 4
S_Z2 = S_H + 4
S_X2 = S_Z2 + 15
S_XF = S_X2 + 3
S_OC = S_XF + 4
S_PX = S_OC + 2
S_PZ = S_PX + 3
S_PY = S_PZ + 15
N_SEM = S_PY + 1


def pick(rows, cols, source):
    r = lax.broadcasted_iota(jnp.int32, (rows, 1), 0)
    c = lax.broadcasted_iota(jnp.int32, (rows, cols), 1)
    return jnp.where(c == source(r), 1.0, 0.0).astype(BF)


def dot(a, b):
    return jnp.dot(a, b, preferred_element_type=F32)


def dot_nt(a, b):
    return lax.dot_general(a, b, (((1,), (1,)), ((), ())), preferred_element_type=F32)


def dot_tn(a, b):
    return lax.dot_general(a, b, (((0,), (0,)), ((), ())), preferred_element_type=F32)


def mod(a, n):
    return lax.rem(a + n, n)


def kernel(
    in_hbm, cot_hbm, mod_hbm, qkv_hbm, proj_hbm, qg_hbm, kg_hbm,
    out_ref, ig_ref, pg_ref,
    in_ref, cot_ref, mod_ref, qkv_ref, proj_ref, qg_ref, kg_ref,
    order, perm, w_in, rows_in, r1, w4, z1, r2, xw, a, bp, bq, bt, bu, hp, hq, ht, hu, zb, r3, xs, r4, px, pxr, pz, pzr, pgs,
    ss, rs, ls,
):
    fetches = [
        pltpu.make_async_copy(src, dst, ls.at[i])
        for i, (src, dst) in enumerate(
            [
                (qkv_hbm, qkv_ref), (proj_hbm, proj_ref), (in_hbm, in_ref), (cot_hbm, cot_ref),
                (mod_hbm, mod_ref), (qg_hbm, qg_ref), (kg_hbm, kg_ref),
            ]
        )
    ]
    for fetch in fetches:
        fetch.start()

    f, hd, dp = lax.axis_index("frame"), lax.axis_index("head"), lax.axis_index("dp")
    z, x = f // NX, lax.rem(f, NX)
    core, y = lax.rem(hd, 2), (hd // 2) * 2 + dp
    far_hd = mod(hd + 2, 4)

    def at_x(d):
        return (z * NX + mod(x + d, NX), hd, dp)

    def at_x_far(d):
        return (z * NX + mod(x + d, NX), far_hd, dp)

    def at_zx(dz, dx):
        return (mod(z + dz, NZ) * NX + mod(x + dx, NX), hd, dp)

    def at_z(d):
        return (mod(z + d, NZ) * NX + x, hd, dp)

    def at_y(d):
        yy = mod(y + d, NY)
        return (f, (yy // 2) * 2 + core, lax.rem(yy, 2))

    across = (f, hd + 1 - 2 * core, dp)

    def copy(src, dst, i, dev):
        return pltpu.make_async_remote_copy(
            src_ref=src, dst_ref=dst, send_sem=ss.at[i], recv_sem=rs.at[i], device_id=dev, device_id_type=MESH
        )

    sent = []

    def send(*args):
        c = copy(*args)
        c.start()
        sent.append(c.wait_send)

    def landed(ref, i):
        copy(ref, ref, i, across).wait_recv()

    def z_send(src_of, dst, base):
        def each(d, c):
            copy(src_of(mod(z + d, NZ)), dst.at[z], base + d - 1, at_z(d)).start()
            return c

        lax.fori_loop(1, NZ, each, 0)

        def each_sent(d, c):
            copy(src_of(mod(z + d, NZ)), dst.at[z], base + d - 1, at_z(d)).wait_send()
            return c

        sent.append(lambda: lax.fori_loop(1, NZ, each_sent, 0))

    def z_landed(dst, base):
        def each(d, c):
            landed(dst.at[mod(z - d, NZ)], base + d - 1)
            return c

        lax.fori_loop(1, NZ, each, 0)

    routes = [(-2, 3), (1, 1), (-1, 3), (0, 1), (2, 1), (0, 3), (-1, 1), (1, 3), (2, 0), (1, 0), (-1, 0)]
    barrier = pltpu.get_barrier_semaphore()

    def greet(dev):
        pl.semaphore_signal(barrier, inc=1, device_id=dev, device_id_type=MESH)

    with jax.named_scope("greet"):

        def greet_z(d, c):
            greet(at_z(d))
            return c

        lax.fori_loop(1, NZ, greet_z, 0)
        for d in range(1, NX):
            greet(at_x(d))
            greet(at_x_far(d))
        for dz, dx in routes:
            if dx and dz:
                greet(at_zx(dz, dx))
        for d in range(1, NY):
            greet(at_y(d))
        greet(across)

    def mean(v):
        return jnp.sum(v, axis=1, keepdims=True) * (1.0 / v.shape[1])

    def normalise():
        v = in_ref[...].astype(F32)
        v = v - mean(v)
        root = lax.rsqrt(mean(v * v) + 1e-06)
        return v * root, root

    with jax.named_scope("weights"):
        for fetch in fetches:
            fetch.wait()
        blocks = [qkv_ref[w].astype(F32) for w in range(3)] + [proj_ref[...].astype(F32)]
        w_all = jnp.concatenate([jnp.where(dp == 0, v[:, :144], v[:, 144:]) for v in blocks], axis=1)
        tail = jnp.concatenate([w_all[16:18, HD * g : HD * g + HD] for g in range(8)], axis=0)
        w_in[...] = jnp.concatenate([w_all[:16], tail], axis=1).astype(BF)

    with jax.named_scope("rows"):
        feature = lax.broadcasted_iota(jnp.int32, (1152, QF), 0)
        col = lax.broadcasted_iota(jnp.int32, (1, QF), 1)
        b, k = lax.div(col, GF), lax.rem(col, GF)
        from_col = jnp.where(k < 64, (k >> 4) * 288 + (k & 15), ((k - 64) >> 1) * 288 + 16 + (k & 1)) + b * 72
        from_col = jnp.where(k < 72, from_col, -100)
        for q in range(4):
            order[q] = jnp.where(feature == from_col + 18 * q, 1.0, 0.0).astype(BF)
        perm[0] = pick(256, 256, lambda r: ((r >> 1) & 1) * 128 + (r >> 4) * 8 + ((r >> 2) & 3) * 2 + (r & 1))
        perm[1] = pick(256, 256, lambda r: ((r >> 1) & 15) * 16 + (r >> 6) * 4 + ((r >> 5) & 1) * 2 + (r & 1))
        perm[2] = pick(256, 256, lambda r: ((r >> 1) & 1) * 128 + ((r >> 2) & 3) * 32 + (r >> 4) * 2 + (r & 1))
        perm[3] = pick(256, 256, lambda r: ((r >> 1) & 3) * 64 + (r >> 7) * 32 + ((r >> 3) & 15) * 2 + (r & 1))
        normed, _ = normalise()
        hidden_in = (normed * (1.0 + mod_ref[1:2]) + mod_ref[0:1]).astype(BF)
        d_branch = (mod_ref[2:3] * cot_ref[...].astype(F32)).astype(BF)
        quarter = dot(jnp.concatenate([hidden_in, d_branch], axis=0), order[hd]).astype(BF)
        rows_in[...] = dot(perm[0], quarter).astype(BF).reshape(NZ, 16, QF)

    with jax.named_scope("greeted"):
        pl.semaphore_wait(barrier, 31)

    zq = mod(z, 4)

    def send_near(lo, hi):
        for i in range(lo, hi):
            send(xw.at[x, zq], xw.at[x, zq], S_WX + i, at_zx(*routes[i]))

    def near_landed(i):
        dz, dx = routes[i]
        slot = xw.at[mod(x - dx, NX), mod(z - dz, 4)]
        landed(slot, S_WX + i)
        return slot

    with jax.named_scope("rows_z"):
        z_send(lambda k: rows_in.at[k], r2, S_Z1)
        for i, d in enumerate((8, 4, -4)):
            send(w_in, w4.at[z // 4], S_W4 + i, at_z(d))
        r2[z] = rows_in[z]
        w4[z // 4] = w_in[...]
        z_landed(r2, S_Z1)
        z1[...] = dot(perm[1], r2[...].reshape(256, QF)).astype(BF).reshape(NX, 64, QF)
        for d in (2, 1, 3):
            send(z1.at[mod(x + d, NX)], r1.at[x], S_X1 + d - 1, at_x(d))
        r1[x] = z1[x]

    with jax.named_scope("weights_4"):
        for i, d in enumerate((8, 4, -4)):
            landed(w4.at[mod(z // 4 - d // 4, 4)], S_W4 + i)
        tail = w4[:, :, WCOLS : WCOLS + HD].reshape(64, HD)
        tail = jnp.concatenate([tail] * 8, axis=1)
        pair = (lax.broadcasted_iota(jnp.int32, (64, WCOLS), 0) >> 1) & 7
        group = lax.div(lax.broadcasted_iota(jnp.int32, (1, WCOLS), 1), HD)
        tail = jnp.where(pair == group, tail.astype(F32), 0.0).astype(BF)
        r = lax.broadcasted_iota(jnp.int32, (16, 64), 0)
        c = lax.broadcasted_iota(jnp.int32, (16, 64), 1)
        gather = jnp.where(r == (c >> 4) * 2 + (c & 1), 1.0, 0.0).astype(BF)
        xw[x, zq, 0:64] = w4[:, :, 0:WCOLS].reshape(64, WCOLS)
        xw[x, zq, 64:80] = dot(gather, tail).astype(BF)
        send_near(0, 8)

    with jax.named_scope("rows_x"):
        for d in range(1, NX):
            landed(r1.at[mod(x - d, NX)], S_X1 + d - 1)
        for arr in range(2):
            for k in range(NX):
                a[core, y, 128 * arr + 32 * k : 128 * arr + 32 * k + 32] = r1[k, 32 * arr : 32 * arr + 32]
        for d in (2, 1, 3):
            send(a.at[core, y], a.at[core, y], S_AY + d - 1, at_y(d))
        send(a.at[core, y], a.at[core, y], S_AC, across)

    with jax.named_scope("weights_near"):
        send_near(8, len(routes))
        for i in range(4):
            slot = near_landed(i)
            send(slot, slot, S_WX + 11 + i, at_x(routes[i][1] if routes[i][1] == 1 else -1))

    with jax.named_scope("rows_y"):
        for d in (1, 3, 2):
            slot = a.at[core, mod(y - d, NY)]
            landed(slot, S_AY + d - 1)
            send(slot, slot, S_AC + d, across)
        for d in range(NY):
            landed(a.at[1 - core, mod(y - d, NY)], S_AC + d)

    def rows_of(q, arr):
        lo = arr * 128
        return jnp.concatenate([a[q % 2, (q // 2) * 2 + p, lo : lo + 128, :] for p in range(2)], axis=0)

    with jax.named_scope("project"):

        def weights(q):
            return xw[q].reshape(QF, WCOLS)

        def project(q):
            w = weights(q)
            return dot(rows_of(q, 0), w[:, :QKV]), dot(rows_of(q, 1), w[:, QKV:])

        raw, d_att = jnp.zeros((256, QKV), F32), jnp.zeros((256, 144), F32)
        for dx in (1, 3, 0, 2):
            q = mod(x - dx, NX)
            for i in range(4, len(routes)):
                if routes[i][1] == dx:
                    near_landed(i)
            if dx == 2:
                for i in range(4):
                    landed(xw.at[q, mod(z - routes[i][0], 4)], S_WX + 11 + i)
            more_raw, more_d = project(q)
            raw, d_att = raw + more_raw, d_att + more_d
        d_att = d_att.astype(BF)

    q_gain, k_gain = qg_ref[...], kg_ref[...]
    factor = 1.0 / np.sqrt(np.float32(HD))
    row_i = lax.broadcasted_iota(jnp.int32, (128, 128), 0) % 2
    col_i = lax.broadcasted_iota(jnp.int32, (128, 128), 1) % 2
    same = row_i == col_i

    def norm(v, gain):
        root = lax.rsqrt(jnp.sum(v * v, axis=-1, keepdims=True) * (1.0 / HD) + 1e-06)
        return (v * root * gain).astype(BF), root

    def part_cols(v, p, k):
        return v[128 * p : 128 * p + 128, HD * k : HD * k + HD]

    with jax.named_scope("attend"):
        state, att = [], [[], []]
        for p in range(2):
            for h in range(2):
                rq, rk, v = (part_cols(raw, p, 2 * w + h) for w in range(3))
                v = v.astype(BF)
                qn, root_q = norm(rq, q_gain)
                kn, root_k = norm(rk, k_gain)
                s = jnp.where(same, dot_nt(qn, kn) * factor, -1e30)
                e = jnp.exp(s - jnp.max(s, axis=-1, keepdims=True))
                pr = e / jnp.sum(e, axis=-1, keepdims=True)
                pb = pr.astype(BF)
                att[p].append(dot(pb, v).astype(BF))
                state.append((rq, rk, v, qn, kn, root_q, root_k, pr, pb))
        att = [jnp.concatenate(half, axis=1) for half in att]

    def spread(q, val, buf):
        for p in range(2):
            buf[q % 2, (q // 2) * 2 + p] = val[128 * p : 128 * p + 128].astype(BF)

    with jax.named_scope("branch"):
        both = jnp.concatenate(att, axis=0)
        for q in range(4):
            spread(q, dot_nt(both, weights(q)[:, QKV:]), bp)
        send(bp.at[1 - core], bq, S_B, across)

    def to_y(own, got, total, far, base):
        landed(got, base)
        total[...] = (own[core].astype(F32) + got[...].astype(F32)).astype(BF)
        for d in (2, 1, 3):
            send(total.at[mod(y + d, NY)], far.at[d - 1], base + d, at_y(d))

    def y_sum(total, far, base):
        for d in range(1, NY):
            landed(far.at[d - 1], base + d)
        s = total[y].astype(F32)
        for d in range(1, NY):
            s += far[d - 1].astype(F32)
        return s

    with jax.named_scope("branch_y"):
        to_y(bp, bq, bt, bu, S_B)

    with jax.named_scope("attend_back"):
        d_raw = []
        for p in range(2):
            cols_q, cols_k, cols_v = [], [], []
            for h in range(2):
                rq, rk, v, qn, kn, root_q, root_k, pr, pb = state[2 * p + h]
                da = part_cols(d_att, p, h)
                dv = dot_tn(pb, da).astype(BF)
                d_p = dot_nt(da, v)
                ds = (pr * (d_p - jnp.sum(pr * d_p, axis=-1, keepdims=True)) * factor).astype(BF)
                dq = dot(ds, kn).astype(BF)
                dk = dot_tn(ds, qn).astype(BF)

                def norm_back(v_raw, root, gain, d_n):
                    gq = gain * d_n.astype(F32)
                    inner = jnp.sum(v_raw * gq, axis=-1, keepdims=True) * (1.0 / HD)
                    return (root * gq - v_raw * (root * root * root) * inner).astype(BF)

                cols_q.append(norm_back(rq, root_q, q_gain, dq))
                cols_k.append(norm_back(rk, root_k, k_gain, dk))
                cols_v.append(dv)
            d_raw.append(jnp.concatenate(cols_q + cols_k + cols_v, axis=1))
        d_raw = jnp.concatenate(d_raw, axis=0)
        for k in range(4):
            q = mod(1 - core, 2) + 2 * k if k < 2 else core + 2 * (k - 2)
            spread(q, dot_nt(d_raw, weights(q)[:, :QKV]), hp)
            if k == 1:
                send(hp.at[1 - core], hq, S_H, across)

    with jax.named_scope("proj_grad"):
        none = jnp.zeros((128, 144), BF)
        att_c = jnp.concatenate(
            [jnp.concatenate([att[0], none], axis=1), jnp.concatenate([none, att[1]], axis=1)], axis=0
        )
        for q in range(4):
            px[q] = dot_tn(rows_of(q, 1), att_c).astype(BF)
        for d in (2, 1, 3):
            send(px.at[mod(x + d, NX)], pxr.at[d - 1], S_PX + d - 1, at_x(d))

    with jax.named_scope("hidden_y"):
        to_y(hp, hq, ht, hu, S_H)

    with jax.named_scope("back_z"):
        branch = y_sum(bt, bu, S_B)
        hidden = y_sum(ht, hu, S_H)
        both = jnp.concatenate([branch.astype(BF), hidden.astype(BF)], axis=0)
        zb[...] = dot(perm[2], both).astype(BF).reshape(NZ, 16, QF)
        z_send(lambda k: zb.at[k], r3, S_Z2)
        r3[z] = zb[z]

    with jax.named_scope("grad_x"):
        for d in range(1, NX):
            landed(pxr.at[d - 1], S_PX + d - 1)
        s = px[x].astype(F32)
        for d in range(1, NX):
            s += pxr[d - 1].astype(F32)
        body = jnp.concatenate([s[GF * b : GF * b + 64] for b in range(4)], axis=0)
        tail = jnp.concatenate([s[GF * b + 64 : GF * b + 72] for b in range(4)], axis=0).astype(BF)
        widen = pick(256, 32, lambda r: jnp.where((r & 15) < 8, (r >> 4) * 2 + ((r >> 2) & 1), -1))
        row4 = lax.broadcasted_iota(jnp.int32, (256, 288), 0) & 3
        group = lax.div(lax.broadcasted_iota(jnp.int32, (1, 288), 1), HD)
        tail = jnp.where(row4 == group, dot(widen, tail), 0.0)
        tail = tail[:, 0:72] + tail[:, 72:144] + tail[:, 144:216] + tail[:, 216:288]
        pz[...] = jnp.concatenate([body, tail], axis=1).astype(BF).reshape(NZ, 16, 360)
        z_send(lambda k: pz.at[lax.rem(k, 4) * 4 + k // 4], pzr, S_PZ)
        pzr[z] = pz[zq * 4 + z // 4]

    def natural(q):
        return dot_nt(dot(perm[3], r4[q].reshape(256, QF)).astype(BF), order[q])

    with jax.named_scope("back_x"):
        z_landed(r3, S_Z2)
        xs[...] = dot(perm[1], r3[...].reshape(256, QF)).astype(BF).reshape(NX, 64, QF)
        for d in (2, 1, 3):
            to = mod(x + d, NX)
            send(xs.at[to], r4.at[hd, x], S_XF + d, at_x_far(d))
            send(xs.at[to], r4.at[hd, x], S_X2 + d - 1, at_x(d))
        send(xs.at[x], r4.at[hd, x], S_XF, at_y(2))
        r4[hd, x] = xs[x]
        for d in range(1, NX):
            landed(r4.at[hd, mod(x - d, NX)], S_X2 + d - 1)
        send(r4.at[hd], r4.at[hd], S_OC, across)
        normed, root = normalise()
        total = natural(hd)
        for d in range(NX):
            landed(r4.at[far_hd, mod(x - d, NX)], S_XF + d)
        send(r4.at[far_hd], r4.at[far_hd], S_OC + 1, across)
        total += natural(far_hd)

    with jax.named_scope("grad_z"):
        z_landed(pzr, S_PZ)
        s = pzr[0].astype(F32)
        for k in range(1, NZ):
            s += pzr[k].astype(F32)
        pgs[dp] = s
        send(pgs.at[dp], pgs.at[dp], S_PY, at_y(1 - 2 * dp))

    with jax.named_scope("results"):
        landed(r4.at[hd + 1 - 2 * core], S_OC)
        total += natural(hd + 1 - 2 * core)
        landed(r4.at[mod(hd + 3 - 2 * core, 4)], S_OC + 1)
        total += natural(mod(hd + 3 - 2 * core, 4))
        out_ref[...] = (in_ref[...].astype(F32) + mod_ref[2:3] * total[0:128]).astype(BF)
        d_n = total[128:256] * (1.0 + mod_ref[1:2])
        d_in = root * (d_n - mean(d_n) - normed * mean(d_n * normed))
        ig_ref[...] = (cot_ref[...].astype(F32) + d_in).astype(BF)
        landed(pgs.at[1 - dp], S_PY)
        halves = []
        for v in (pgs[0], pgs[1]):
            last = [
                jnp.concatenate([jnp.concatenate([v[r + k : r + k + 1, 288:360] for k in range(2)], axis=1) for r in (o, o + 4)], axis=0)
                for o in (0, 2)
            ]
            parts = [jnp.concatenate([v[:, 144 * p : 144 * p + 144], last[p]], axis=0) for p in range(2)]
            halves.append(jnp.where(dp == 0, parts[0], parts[1]))
        pg_ref[0:18, 0:288] = jnp.concatenate(halves, axis=1)

    with jax.named_scope("sent"):
        for wait in sent:
            wait()


def per_device(inputs, modulation, qkv_weight, proj_weight, q_gain, k_gain, cotangent):
    tokens, width = inputs.shape[1:]

    def vm(*shape, dtype=BF):
        return pltpu.VMEM(shape, dtype)

    operands = (inputs[0], cotangent[0], modulation, qkv_weight, proj_weight.T, q_gain[None], k_gain[None])
    out, ig, pg = pl.pallas_call(
        kernel,
        out_shape=(
            jax.ShapeDtypeStruct((tokens, width), BF),
            jax.ShapeDtypeStruct((tokens, width), BF),
            jax.ShapeDtypeStruct((24, 384), F32),
        ),
        in_specs=[pl.BlockSpec(memory_space=pl.ANY)] * 7,
        out_specs=[pl.BlockSpec(memory_space=pltpu.VMEM)] * 3,
        scratch_shapes=[
            *[vm(*v.shape, dtype=v.dtype) for v in operands],
            vm(4, 1152, QF),
            vm(4, 256, 256),
            vm(16, WCOLS + HD),
            vm(NZ, 16, QF),
            vm(NX, 64, QF),
            vm(4, 16, WCOLS + HD),
            vm(NX, 64, QF),
            vm(NZ, 16, QF),
            vm(NX, 4, GF, WCOLS),
            vm(2, NY, 256, QF),
            vm(2, NY, 128, QF),
            vm(NY, 128, QF),
            vm(NY, 128, QF),
            vm(3, 128, QF),
            vm(2, NY, 128, QF),
            vm(NY, 128, QF),
            vm(NY, 128, QF),
            vm(3, 128, QF),
            vm(NZ, 16, QF),
            vm(NZ, 16, QF),
            vm(NX, 64, QF),
            vm(4, NX, 64, QF),
            vm(NX, QF, 288),
            vm(3, QF, 288),
            vm(NZ, 16, 360),
            vm(NZ, 16, 360),
            vm(2, 16, 360, dtype=F32),
            pltpu.SemaphoreType.DMA((N_SEM,)),
            pltpu.SemaphoreType.DMA((N_SEM,)),
            pltpu.SemaphoreType.DMA((len(operands),)),
        ],
        compiler_params=pltpu.CompilerParams(
            collective_id=0, has_side_effects=True, vmem_limit_bytes=60 * 1024 * 1024
        ),
    )(*operands)

    return out[None], ig[None], pg[:18, :288].T


def solution(mesh):
    return jax.shard_map(
        per_device,
        mesh=mesh,
        in_specs=(
            P(("dp", "frame"), None, None),
            P("dp", None),
            P(None, "frame", "head"),
            P("head", "frame"),
            P(),
            P(),
            P(("dp", "frame"), None, None),
        ),
        out_specs=(
            P(("dp", "frame"), None, None),
            P(("dp", "frame"), None, None),
            P(("dp", "head"), "frame"),
        ),
        check_vma=False,
    )
```

```python
import jax
import jax.numpy as jnp
import numpy as np
from jax import lax
from jax.experimental import pallas as pl
from jax.experimental.pallas import tpu as pltpu
from jax.sharding import PartitionSpec as P

MESH = pl.DeviceIdType.MESH
BF = jnp.bfloat16
F32 = jnp.float32
NZ, NX, NY = 16, 4, 4
HD = 72
GF = 80
QF = 4 * GF
QKV, WCOLS = 432, 576

S_Z1 = 0
S_X1 = S_Z1 + 15
S_W4 = S_X1 + 3
S_WX = S_W4 + 3
S_AY = S_WX + 16
S_AC = S_AY + 3
S_B = S_AC + 4
S_H = S_B + 4
S_Z2 = S_H + 4
S_X2 = S_Z2 + 15
S_XF = S_X2 + 3
S_OC = S_XF + 4
S_PX = S_OC + 2
S_PZ = S_PX + 3
S_PY = S_PZ + 15
N_SEM = S_PY + 1


def pick(rows, cols, source):
    r = lax.broadcasted_iota(jnp.int32, (rows, 1), 0)
    c = lax.broadcasted_iota(jnp.int32, (rows, cols), 1)
    return jnp.where(c == source(r), 1.0, 0.0).astype(BF)


def dot(a, b):
    return jnp.dot(a, b, preferred_element_type=F32)


def dot_nt(a, b):
    return lax.dot_general(a, b, (((1,), (1,)), ((), ())), preferred_element_type=F32)


def dot_tn(a, b):
    return lax.dot_general(a, b, (((0,), (0,)), ((), ())), preferred_element_type=F32)


def mod(a, n):
    return lax.rem(a + n, n)


def kernel(
    in_hbm, cot_hbm, mod_hbm, qkv_hbm, proj_hbm, qg_hbm, kg_hbm,
    out_ref, ig_ref, pg_ref,
    in_ref, cot_ref, mod_ref, qkv_ref, proj_ref, qg_ref, kg_ref,
    order, perm, w_in, rows_in, r1, w4, z1, r2, xw, a, bp, bq, bt, bu, hp, hq, ht, hu, zb, r3, xs, r4, px, pxr, pz, pzr, pgs,
    ss, rs, ls,
):
    fetches = [
        pltpu.make_async_copy(src, dst, ls.at[i])
        for i, (src, dst) in enumerate(
            [
                (qkv_hbm, qkv_ref), (proj_hbm, proj_ref), (in_hbm, in_ref), (cot_hbm, cot_ref),
                (mod_hbm, mod_ref), (qg_hbm, qg_ref), (kg_hbm, kg_ref),
            ]
        )
    ]
    for fetch in fetches:
        fetch.start()

    f, hd, dp = lax.axis_index("frame"), lax.axis_index("head"), lax.axis_index("dp")
    z, x = f // NX, lax.rem(f, NX)
    core, y = lax.rem(hd, 2), (hd // 2) * 2 + dp
    far_hd = mod(hd + 2, 4)

    def at_x(d):
        return (z * NX + mod(x + d, NX), hd, dp)

    def at_x_far(d):
        return (z * NX + mod(x + d, NX), far_hd, dp)

    def at_zx(dz, dx):
        return (mod(z + dz, NZ) * NX + mod(x + dx, NX), hd, dp)

    def at_z(d):
        return (mod(z + d, NZ) * NX + x, hd, dp)

    def at_y(d):
        yy = mod(y + d, NY)
        return (f, (yy // 2) * 2 + core, lax.rem(yy, 2))

    across = (f, hd + 1 - 2 * core, dp)

    def copy(src, dst, i, dev):
        return pltpu.make_async_remote_copy(
            src_ref=src, dst_ref=dst, send_sem=ss.at[i], recv_sem=rs.at[i], device_id=dev, device_id_type=MESH
        )

    sent = []

    def send(*args):
        c = copy(*args)
        c.start()
        sent.append(c.wait_send)

    def landed(ref, i):
        copy(ref, ref, i, across).wait_recv()

    def z_send(src_of, dst, base):
        def each(k, c):
            d = 8 + ((k + 1) // 2) * (1 - 2 * lax.rem(k, 2))
            copy(src_of(mod(z + d, NZ)), dst.at[z], base + d - 1, at_z(d)).start()
            return c

        lax.fori_loop(0, NZ - 1, each, 0)

        def each_sent(d, c):
            copy(src_of(mod(z + d, NZ)), dst.at[z], base + d - 1, at_z(d)).wait_send()
            return c

        sent.append(lambda: lax.fori_loop(1, NZ, each_sent, 0))

    def z_landed(dst, base):
        def each(d, c):
            landed(dst.at[mod(z - d, NZ)], base + d - 1)
            return c

        lax.fori_loop(1, NZ, each, 0)

    routes = [(-2, 3), (1, 1), (-1, 3), (0, 1), (2, 1), (0, 3), (-1, 1), (1, 3), (2, 0), (1, 0), (-1, 0)]
    barrier = pltpu.get_barrier_semaphore()

    def greet(dev):
        pl.semaphore_signal(barrier, inc=1, device_id=dev, device_id_type=MESH)

    with jax.named_scope("greet"):

        def greet_z(d, c):
            greet(at_z(d))
            return c

        lax.fori_loop(1, NZ, greet_z, 0)
        for d in range(1, NX):
            greet(at_x(d))
            greet(at_x_far(d))
        for dz, dx in routes:
            if dx and dz:
                greet(at_zx(dz, dx))
        for d in range(1, NY):
            greet(at_y(d))
        greet(across)

    def mean(v):
        return jnp.sum(v, axis=1, keepdims=True) * (1.0 / v.shape[1])

    def normalise():
        v = in_ref[...].astype(F32)
        v = v - mean(v)
        root = lax.rsqrt(mean(v * v) + 1e-06)
        return v * root, root

    with jax.named_scope("weights"):
        for fetch in fetches:
            fetch.wait()
        blocks = [qkv_ref[w].astype(F32) for w in range(3)] + [proj_ref[...].astype(F32)]
        w_all = jnp.concatenate([jnp.where(dp == 0, v[:, :144], v[:, 144:]) for v in blocks], axis=1)
        tail = jnp.concatenate([w_all[16:18, HD * g : HD * g + HD] for g in range(8)], axis=0)
        w_in[...] = jnp.concatenate([w_all[:16], tail], axis=1).astype(BF)

    with jax.named_scope("rows"):
        feature = lax.broadcasted_iota(jnp.int32, (1152, QF), 0)
        col = lax.broadcasted_iota(jnp.int32, (1, QF), 1)
        b, k = lax.div(col, GF), lax.rem(col, GF)
        from_col = jnp.where(k < 64, (k >> 4) * 288 + (k & 15), ((k - 64) >> 1) * 288 + 16 + (k & 1)) + b * 72
        from_col = jnp.where(k < 72, from_col, -100)
        for q in range(4):
            order[q] = jnp.where(feature == from_col + 18 * q, 1.0, 0.0).astype(BF)
        perm[0] = pick(256, 256, lambda r: ((r >> 1) & 1) * 128 + (r >> 4) * 8 + ((r >> 2) & 3) * 2 + (r & 1))
        perm[1] = pick(256, 256, lambda r: ((r >> 1) & 15) * 16 + (r >> 6) * 4 + ((r >> 5) & 1) * 2 + (r & 1))
        perm[2] = pick(256, 256, lambda r: ((r >> 1) & 1) * 128 + ((r >> 2) & 3) * 32 + (r >> 4) * 2 + (r & 1))
        perm[3] = pick(256, 256, lambda r: ((r >> 1) & 3) * 64 + (r >> 7) * 32 + ((r >> 3) & 15) * 2 + (r & 1))
        normed, _ = normalise()
        hidden_in = (normed * (1.0 + mod_ref[1:2]) + mod_ref[0:1]).astype(BF)
        d_branch = (mod_ref[2:3] * cot_ref[...].astype(F32)).astype(BF)
        quarter = dot(jnp.concatenate([hidden_in, d_branch], axis=0), order[hd]).astype(BF)
        rows_in[...] = dot(perm[0], quarter).astype(BF).reshape(NZ, 16, QF)

    with jax.named_scope("greeted"):
        pl.semaphore_wait(barrier, 31)

    zq = mod(z, 4)

    def send_near(lo, hi):
        for i in range(lo, hi):
            send(xw.at[x, zq], xw.at[x, zq], S_WX + i, at_zx(*routes[i]))

    def near_landed(i):
        dz, dx = routes[i]
        slot = xw.at[mod(x - dx, NX), mod(z - dz, 4)]
        landed(slot, S_WX + i)
        return slot

    with jax.named_scope("rows_z"):
        z_send(lambda k: rows_in.at[k], r2, S_Z1)
        for i, d in enumerate((8, 4, -4)):
            send(w_in, w4.at[z // 4], S_W4 + i, at_z(d))
        r2[z] = rows_in[z]
        w4[z // 4] = w_in[...]
        z_landed(r2, S_Z1)
        z1[...] = dot(perm[1], r2[...].reshape(256, QF)).astype(BF).reshape(NX, 64, QF)
        for d in (2, 1, 3):
            send(z1.at[mod(x + d, NX)], r1.at[x], S_X1 + d - 1, at_x(d))
        r1[x] = z1[x]

    with jax.named_scope("weights_4"):
        for i, d in enumerate((8, 4, -4)):
            landed(w4.at[mod(z // 4 - d // 4, 4)], S_W4 + i)
        tail = w4[:, :, WCOLS : WCOLS + HD].reshape(64, HD)
        tail = jnp.concatenate([tail] * 8, axis=1)
        pair = (lax.broadcasted_iota(jnp.int32, (64, WCOLS), 0) >> 1) & 7
        group = lax.div(lax.broadcasted_iota(jnp.int32, (1, WCOLS), 1), HD)
        tail = jnp.where(pair == group, tail.astype(F32), 0.0).astype(BF)
        r = lax.broadcasted_iota(jnp.int32, (16, 64), 0)
        c = lax.broadcasted_iota(jnp.int32, (16, 64), 1)
        gather = jnp.where(r == (c >> 4) * 2 + (c & 1), 1.0, 0.0).astype(BF)
        xw[x, zq, 0:64] = w4[:, :, 0:WCOLS].reshape(64, WCOLS)
        xw[x, zq, 64:80] = dot(gather, tail).astype(BF)
        send_near(0, 8)

    with jax.named_scope("rows_x"):
        for d in range(1, NX):
            landed(r1.at[mod(x - d, NX)], S_X1 + d - 1)
        for arr in range(2):
            for k in range(NX):
                a[core, y, 128 * arr + 32 * k : 128 * arr + 32 * k + 32] = r1[k, 32 * arr : 32 * arr + 32]
        for d in (2, 1, 3):
            send(a.at[core, y], a.at[core, y], S_AY + d - 1, at_y(d))
        send(a.at[core, y], a.at[core, y], S_AC, across)

    with jax.named_scope("weights_near"):
        send_near(8, len(routes))
        for i in range(4):
            slot = near_landed(i)
            send(slot, slot, S_WX + 11 + i, at_x(routes[i][1] if routes[i][1] == 1 else -1))

    with jax.named_scope("rows_y"):
        for d in (1, 3, 2):
            slot = a.at[core, mod(y - d, NY)]
            landed(slot, S_AY + d - 1)
            send(slot, slot, S_AC + d, across)
        for d in range(NY):
            landed(a.at[1 - core, mod(y - d, NY)], S_AC + d)

    def rows_of(q, arr):
        lo = arr * 128
        return jnp.concatenate([a[q % 2, (q // 2) * 2 + p, lo : lo + 128, :] for p in range(2)], axis=0)

    with jax.named_scope("project"):

        def weights(q):
            return xw[q].reshape(QF, WCOLS)

        def project(q):
            w = weights(q)
            return dot(rows_of(q, 0), w[:, :QKV]), dot(rows_of(q, 1), w[:, QKV:])

        raw, d_att = jnp.zeros((256, QKV), F32), jnp.zeros((256, 144), F32)
        for dx in (1, 3, 0, 2):
            q = mod(x - dx, NX)
            for i in range(4, len(routes)):
                if routes[i][1] == dx:
                    near_landed(i)
            if dx == 2:
                for i in range(4):
                    landed(xw.at[q, mod(z - routes[i][0], 4)], S_WX + 11 + i)
            more_raw, more_d = project(q)
            raw, d_att = raw + more_raw, d_att + more_d
        d_att = d_att.astype(BF)

    q_gain, k_gain = qg_ref[...], kg_ref[...]
    factor = 1.0 / np.sqrt(np.float32(HD))
    row_i = lax.broadcasted_iota(jnp.int32, (128, 128), 0) % 2
    col_i = lax.broadcasted_iota(jnp.int32, (128, 128), 1) % 2
    same = row_i == col_i

    def norm(v, gain):
        root = lax.rsqrt(jnp.sum(v * v, axis=-1, keepdims=True) * (1.0 / HD) + 1e-06)
        return (v * root * gain).astype(BF), root

    def part_cols(v, p, k):
        return v[128 * p : 128 * p + 128, HD * k : HD * k + HD]

    with jax.named_scope("attend"):
        state, att = [], [[], []]
        for p in range(2):
            for h in range(2):
                rq, rk, v = (part_cols(raw, p, 2 * w + h) for w in range(3))
                v = v.astype(BF)
                qn, root_q = norm(rq, q_gain)
                kn, root_k = norm(rk, k_gain)
                s = jnp.where(same, dot_nt(qn, kn) * factor, -1e30)
                e = jnp.exp(s - jnp.max(s, axis=-1, keepdims=True))
                pr = e / jnp.sum(e, axis=-1, keepdims=True)
                pb = pr.astype(BF)
                att[p].append(dot(pb, v).astype(BF))
                state.append((rq, rk, v, qn, kn, root_q, root_k, pr, pb))
        att = [jnp.concatenate(half, axis=1) for half in att]

    def spread(q, val, buf):
        for p in range(2):
            buf[q % 2, (q // 2) * 2 + p] = val[128 * p : 128 * p + 128].astype(BF)

    with jax.named_scope("branch"):
        both = jnp.concatenate(att, axis=0)
        for q in range(4):
            spread(q, dot_nt(both, weights(q)[:, QKV:]), bp)
        send(bp.at[1 - core], bq, S_B, across)

    def to_y(own, got, total, far, base):
        landed(got, base)
        total[...] = (own[core].astype(F32) + got[...].astype(F32)).astype(BF)
        for d in (2, 1, 3):
            send(total.at[mod(y + d, NY)], far.at[d - 1], base + d, at_y(d))

    def y_sum(total, far, base):
        for d in range(1, NY):
            landed(far.at[d - 1], base + d)
        s = total[y].astype(F32)
        for d in range(1, NY):
            s += far[d - 1].astype(F32)
        return s

    with jax.named_scope("branch_y"):
        to_y(bp, bq, bt, bu, S_B)

    with jax.named_scope("attend_back"):
        d_raw = []
        for p in range(2):
            cols_q, cols_k, cols_v = [], [], []
            for h in range(2):
                rq, rk, v, qn, kn, root_q, root_k, pr, pb = state[2 * p + h]
                da = part_cols(d_att, p, h)
                dv = dot_tn(pb, da).astype(BF)
                d_p = dot_nt(da, v)
                ds = (pr * (d_p - jnp.sum(pr * d_p, axis=-1, keepdims=True)) * factor).astype(BF)
                dq = dot(ds, kn).astype(BF)
                dk = dot_tn(ds, qn).astype(BF)

                def norm_back(v_raw, root, gain, d_n):
                    gq = gain * d_n.astype(F32)
                    inner = jnp.sum(v_raw * gq, axis=-1, keepdims=True) * (1.0 / HD)
                    return (root * gq - v_raw * (root * root * root) * inner).astype(BF)

                cols_q.append(norm_back(rq, root_q, q_gain, dq))
                cols_k.append(norm_back(rk, root_k, k_gain, dk))
                cols_v.append(dv)
            d_raw.append(jnp.concatenate(cols_q + cols_k + cols_v, axis=1))
        d_raw = jnp.concatenate(d_raw, axis=0)
        for k in range(4):
            q = mod(1 - core, 2) + 2 * k if k < 2 else core + 2 * (k - 2)
            spread(q, dot_nt(d_raw, weights(q)[:, :QKV]), hp)
            if k == 1:
                send(hp.at[1 - core], hq, S_H, across)

    with jax.named_scope("proj_grad"):
        none = jnp.zeros((128, 144), BF)
        att_c = jnp.concatenate(
            [jnp.concatenate([att[0], none], axis=1), jnp.concatenate([none, att[1]], axis=1)], axis=0
        )
        for q in range(4):
            px[q] = dot_tn(rows_of(q, 1), att_c).astype(BF)
        for d in (2, 1, 3):
            send(px.at[mod(x + d, NX)], pxr.at[d - 1], S_PX + d - 1, at_x(d))

    with jax.named_scope("hidden_y"):
        to_y(hp, hq, ht, hu, S_H)

    with jax.named_scope("back_z"):
        branch = y_sum(bt, bu, S_B)
        hidden = y_sum(ht, hu, S_H)
        both = jnp.concatenate([branch.astype(BF), hidden.astype(BF)], axis=0)
        zb[...] = dot(perm[2], both).astype(BF).reshape(NZ, 16, QF)
        z_send(lambda k: zb.at[k], r3, S_Z2)
        r3[z] = zb[z]

    with jax.named_scope("grad_x"):
        for d in range(1, NX):
            landed(pxr.at[d - 1], S_PX + d - 1)
        s = px[x].astype(F32)
        for d in range(1, NX):
            s += pxr[d - 1].astype(F32)
        body = jnp.concatenate([s[GF * b : GF * b + 64] for b in range(4)], axis=0)
        tail = jnp.concatenate([s[GF * b + 64 : GF * b + 72] for b in range(4)], axis=0).astype(BF)
        widen = pick(256, 32, lambda r: jnp.where((r & 15) < 8, (r >> 4) * 2 + ((r >> 2) & 1), -1))
        row4 = lax.broadcasted_iota(jnp.int32, (256, 288), 0) & 3
        group = lax.div(lax.broadcasted_iota(jnp.int32, (1, 288), 1), HD)
        tail = jnp.where(row4 == group, dot(widen, tail), 0.0)
        tail = tail[:, 0:72] + tail[:, 72:144] + tail[:, 144:216] + tail[:, 216:288]
        pz[...] = jnp.concatenate([body, tail], axis=1).astype(BF).reshape(NZ, 16, 360)
        z_send(lambda k: pz.at[lax.rem(k, 4) * 4 + k // 4], pzr, S_PZ)
        pzr[z] = pz[zq * 4 + z // 4]

    with jax.named_scope("back_x"):
        z_landed(r3, S_Z2)
        xs[...] = dot(perm[1], r3[...].reshape(256, QF)).astype(BF).reshape(NX, 64, QF)
        for d in (2, 1, 3):
            to = mod(x + d, NX)
            send(xs.at[to], r4.at[hd, x], S_XF + d, at_x_far(d))
            send(xs.at[to], r4.at[hd, x], S_X2 + d - 1, at_x(d))
        send(xs.at[x], r4.at[hd, x], S_XF, at_y(2))
        r4[hd, x] = xs[x]
        for d in range(1, NX):
            landed(r4.at[hd, mod(x - d, NX)], S_X2 + d - 1)
        send(r4.at[hd], r4.at[hd], S_OC, across)
        for d in range(NX):
            landed(r4.at[far_hd, mod(x - d, NX)], S_XF + d)
        send(r4.at[far_hd], r4.at[far_hd], S_OC + 1, across)

    with jax.named_scope("grad_z"):
        z_landed(pzr, S_PZ)
        s = pzr[0].astype(F32)
        for k in range(1, NZ):
            s += pzr[k].astype(F32)
        pgs[dp] = s
        send(pgs.at[dp], pgs.at[dp], S_PY, at_y(1 - 2 * dp))

    with jax.named_scope("results"):

        def natural(q):
            return dot_nt(dot(perm[3], r4[q].reshape(256, QF)).astype(BF), order[q])

        normed, root = normalise()
        total = natural(hd) + natural(far_hd)
        landed(r4.at[hd + 1 - 2 * core], S_OC)
        total += natural(hd + 1 - 2 * core)
        landed(r4.at[mod(hd + 3 - 2 * core, 4)], S_OC + 1)
        total += natural(mod(hd + 3 - 2 * core, 4))
        out_ref[...] = (in_ref[...].astype(F32) + mod_ref[2:3] * total[0:128]).astype(BF)
        d_n = total[128:256] * (1.0 + mod_ref[1:2])
        d_in = root * (d_n - mean(d_n) - normed * mean(d_n * normed))
        ig_ref[...] = (cot_ref[...].astype(F32) + d_in).astype(BF)
        landed(pgs.at[1 - dp], S_PY)
        halves = []
        for v in (pgs[0], pgs[1]):
            last = [
                jnp.concatenate([jnp.concatenate([v[r + k : r + k + 1, 288:360] for k in range(2)], axis=1) for r in (o, o + 4)], axis=0)
                for o in (0, 2)
            ]
            parts = [jnp.concatenate([v[:, 144 * p : 144 * p + 144], last[p]], axis=0) for p in range(2)]
            halves.append(jnp.where(dp == 0, parts[0], parts[1]))
        pg_ref[0:18, 0:288] = jnp.concatenate(halves, axis=1)

    with jax.named_scope("sent"):
        for wait in sent:
            wait()


def per_device(inputs, modulation, qkv_weight, proj_weight, q_gain, k_gain, cotangent):
    tokens, width = inputs.shape[1:]

    def vm(*shape, dtype=BF):
        return pltpu.VMEM(shape, dtype)

    operands = (inputs[0], cotangent[0], modulation, qkv_weight, proj_weight.T, q_gain[None], k_gain[None])
    out, ig, pg = pl.pallas_call(
        kernel,
        out_shape=(
            jax.ShapeDtypeStruct((tokens, width), BF),
            jax.ShapeDtypeStruct((tokens, width), BF),
            jax.ShapeDtypeStruct((24, 384), F32),
        ),
        in_specs=[pl.BlockSpec(memory_space=pl.ANY)] * 7,
        out_specs=[pl.BlockSpec(memory_space=pltpu.VMEM)] * 3,
        scratch_shapes=[
            *[vm(*v.shape, dtype=v.dtype) for v in operands],
            vm(4, 1152, QF),
            vm(4, 256, 256),
            vm(16, WCOLS + HD),
            vm(NZ, 16, QF),
            vm(NX, 64, QF),
            vm(4, 16, WCOLS + HD),
            vm(NX, 64, QF),
            vm(NZ, 16, QF),
            vm(NX, 4, GF, WCOLS),
            vm(2, NY, 256, QF),
            vm(2, NY, 128, QF),
            vm(NY, 128, QF),
            vm(NY, 128, QF),
            vm(3, 128, QF),
            vm(2, NY, 128, QF),
            vm(NY, 128, QF),
            vm(NY, 128, QF),
            vm(3, 128, QF),
            vm(NZ, 16, QF),
            vm(NZ, 16, QF),
            vm(NX, 64, QF),
            vm(4, NX, 64, QF),
            vm(NX, QF, 288),
            vm(3, QF, 288),
            vm(NZ, 16, 360),
            vm(NZ, 16, 360),
            vm(2, 16, 360, dtype=F32),
            pltpu.SemaphoreType.DMA((N_SEM,)),
            pltpu.SemaphoreType.DMA((N_SEM,)),
            pltpu.SemaphoreType.DMA((len(operands),)),
        ],
        compiler_params=pltpu.CompilerParams(
            collective_id=0, has_side_effects=True, vmem_limit_bytes=60 * 1024 * 1024
        ),
    )(*operands)

    return out[None], ig[None], pg[:18, :288].T


def solution(mesh):
    return jax.shard_map(
        per_device,
        mesh=mesh,
        in_specs=(
            P(("dp", "frame"), None, None),
            P("dp", None),
            P(None, "frame", "head"),
            P("head", "frame"),
            P(),
            P(),
            P(("dp", "frame"), None, None),
        ),
        out_specs=(
            P(("dp", "frame"), None, None),
            P(("dp", "frame"), None, None),
            P(("dp", "head"), "frame"),
        ),
        check_vma=False,
    )
```
